256 devices in a mesh: dp: 8 (over z), ctx: 32 (over y, x, core).
Axes of the slice: x: 4, y: 4, z: 8, core: 2. Of those that a mesh axis runs over, the one named last changes fastest.
Arguments:
- inputs: bfloat16 [8, 4096, 3072], P('dp', 'ctx'), may hold values from -0.0625 to 0.0625
- queries: bfloat16 [8, 4096, 4096], P('dp', 'ctx'), may hold values from -0.625 to 0.625
- keys: bfloat16 [8, 4096, 4096], P('dp', 'ctx'), may hold values from -0.625 to 0.625
- values: bfloat16 [8, 4096, 4096], P('dp', 'ctx'), may hold values from -0.625 to 0.625
- out_grad: bfloat16 [8, 4096, 4096], P('dp', 'ctx'), may hold values from -0.625 to 0.625
- log_gate: float32 [8, 32, 4096], P('dp', None, 'ctx'), may hold values from -1 to 0
- boundaries: int32 [8, 4], P('dp'), may hold values from 1 to 4095, as said below
Outputs:
- query_grad: bfloat16 [8, 4096, 4096], P('dp', 'ctx')
- key_grad: bfloat16 [8, 4096, 4096], P('dp', 'ctx')
- value_weight_grad: float32 [3072, 4096], P('ctx', 'dp')
The draws below stay inside these ranges and needn't reach their ends.
Inputs may be any that keep to these rules, and one draw needn't show every extreme that they name: `boundaries`: boundary j of a sequence (counting from 0) lies between j * 1024 + 1 and j * 1024 + 1023.
All inputs are finite; a program needn't handle non-finite values.
Results may differ from the reference program's by a relative error of at most 0.034.
Values may be sent and summed in bfloat16 or wider, within the bound.
No kernel may reach another device: no remote copies, remote signals or barrier semaphores. Data moves between devices by JAX's collectives and lax.ppermute only.
A program may use at most 192 MiB of HBM per device.

```python
import jax
import jax.numpy as jnp
from jax import lax

HEADS = 32
HEAD = 128
DIM = 3072
TOK_DEV = 128
BOUNDS = 4
SEQUENCE_LENGTH = 4096
SEQUENCE_COUNT = 8
SEGMENT = 1024
N_CTX = 32


def draw_log_gate(key, part):
    key = jax.random.fold_in(key, 7)
    random_subkeys = jax.random.split(key, 7)
    blocks = SEQUENCE_LENGTH // TOK_DEV
    head_shape = (SEQUENCE_COUNT, HEADS, 1)
    fast_share = 0.5
    quick_decay = jax.random.uniform(random_subkeys[0], head_shape) < fast_share
    fast_rate = jnp.exp(jax.random.uniform(random_subkeys[1], head_shape, minval=jnp.log(1.0 / 50.0), maxval=jnp.log(1.0 / 30.0)))
    slow_rate = jnp.exp(jax.random.uniform(random_subkeys[2], head_shape, minval=jnp.log(0.05), maxval=jnp.log(0.5))) / SEQUENCE_LENGTH
    baseline_decay_rate = jnp.where(quick_decay, fast_rate, slow_rate)
    block_factor = jnp.exp(jax.random.uniform(random_subkeys[3], (SEQUENCE_COUNT, HEADS, blocks), minval=jnp.log(0.5), maxval=jnp.log(2.0)))
    step_factor = jnp.exp(jax.random.uniform(random_subkeys[4], (SEQUENCE_COUNT, HEADS, SEQUENCE_LENGTH), minval=jnp.log(0.5), maxval=jnp.log(2.0)))
    decay_multiplier = jnp.repeat(block_factor, TOK_DEV, axis=2) * step_factor
    reset_position = jax.random.randint(random_subkeys[5], (SEQUENCE_COUNT, 1, 1, 3), 0, SEQUENCE_LENGTH)
    reset_locations = jnp.arange(SEQUENCE_LENGTH, dtype=jnp.int32)[None, None, :, None]
    reset_flags = jnp.minimum(jnp.sum((reset_locations == reset_position).astype(jnp.float32), axis=3), 1.0)
    loss_fraction = jax.random.uniform(random_subkeys[6], (SEQUENCE_COUNT, HEADS, SEQUENCE_LENGTH), minval=0.2, maxval=0.4)
    reset_event = jnp.where(quick_decay, 0.0, reset_flags * jnp.log(1.0 - loss_fraction))
    return (-baseline_decay_rate * decay_multiplier + reset_event).astype(jnp.float32)


def draw_boundaries(key, part):
    key = jax.random.fold_in(key, 3)
    offsets = jax.random.randint(key, (SEQUENCE_COUNT, BOUNDS), 1, SEGMENT)
    starts = jnp.arange(BOUNDS, dtype=jnp.int32) * SEGMENT
    return (starts[None, :] + offsets).astype(jnp.int32)


def raised(values, stream_key, source, target, blocks, factor):
    owner, partner = [(jnp.arange(values.shape[position]) // (values.shape[position] // blocks)).reshape([-1 if axis == position else 1 for axis in range(values.ndim)]) for position in (source, target)]
    chosen = jax.random.permutation(stream_key, blocks)[partner]
    strong = (owner == chosen) | (owner == (partner + blocks // 2) % blocks)
    return jnp.where(strong, factor * values, values)


def block_levels(key, extent, cuts, low, largest):
    gain, own = 1.0, jax.random.fold_in(key, 6)
    for position, shards_of in cuts:
        steps = jnp.exp(jax.random.uniform(jax.random.fold_in(own, position), (shards_of,), jnp.float32, low / len(cuts), largest / len(cuts)))
        gain = gain * jnp.repeat(steps, extent[position] // shards_of).reshape([-1 if axis == position else 1 for axis in range(len(extent))])
    return gain


def scatter_about(rng, extent, spread, reach, shards=(), held_as=jnp.bfloat16):
    values = spread * jax.random.normal(rng, extent, jnp.float32)
    if shards:
        values = values * block_levels(rng, extent, shards, -0.22, 0.18)
    return jnp.clip(values, -reach, reach).astype(held_as)


def bell_draw_with(rng, extent, spread, bound, cuts, heavy, held_as=jnp.bfloat16):
    values = spread * jax.random.normal(rng, extent, jnp.float32)
    if cuts:
        values = values * block_levels(rng, extent, cuts, -0.22, 0.18)
    return jnp.clip(raised(values, jax.random.fold_in(rng, 3), *heavy), -bound, bound).astype(held_as)


def setup_inputs(seed: int = 0) -> dict:
    key_of = jax.random.split(jax.random.key(seed), 8)
    inputs = bell_draw_with(key_of[0], (SEQUENCE_COUNT, SEQUENCE_LENGTH, DIM), ((SEQUENCE_COUNT * SEQUENCE_LENGTH) ** -0.5), 0.0625, ((0, 8), (1, 32)), (1, 2, 32, 2.75))
    queries = scatter_about(key_of[1], (SEQUENCE_COUNT, SEQUENCE_LENGTH, HEADS * HEAD), ((HEAD * SEQUENCE_LENGTH) ** (-1.0 / 6)), 0.625, ((0, 8), (1, 32)))
    keys = scatter_about(key_of[2], (SEQUENCE_COUNT, SEQUENCE_LENGTH, HEADS * HEAD), ((HEAD * SEQUENCE_LENGTH) ** (-1.0 / 6)), 0.625, ((0, 8), (1, 32)))
    values = scatter_about(key_of[3], (SEQUENCE_COUNT, SEQUENCE_LENGTH, HEADS * HEAD), ((HEAD * SEQUENCE_LENGTH) ** (-1.0 / 6)), 0.625, ((0, 8), (1, 32)))
    out_grad = scatter_about(key_of[4], (SEQUENCE_COUNT, SEQUENCE_LENGTH, HEADS * HEAD), ((HEAD * SEQUENCE_LENGTH) ** (-1.0 / 6)), 0.625, ((0, 8), (1, 32)))
    log_gate = draw_log_gate(jax.random.fold_in(key_of[7], 71), 0)
    boundaries = draw_boundaries(jax.random.fold_in(key_of[7], 71), 0)
    return dict(inputs=inputs, queries=queries, keys=keys, values=values, out_grad=out_grad, log_gate=log_gate, boundaries=boundaries)


def rounded(value):
    return lax.optimization_barrier(value.astype(jnp.bfloat16)).astype(jnp.float32)


def block_tables(log_decay, positions, bounds):
    segment_ids = jnp.sum((bounds[None, :] <= positions[:, None]).astype(jnp.int32), axis=1)
    segment_in = jnp.sum((bounds <= positions[0] - 1).astype(jnp.int32))
    cumulative = jnp.cumsum(log_decay, axis=1)
    enter_weight = jnp.where((segment_ids == segment_in)[None, :], jnp.exp(cumulative), 0.0)
    leave_weight = jnp.where((segment_ids == segment_ids[-1])[None, :], jnp.exp(cumulative[:, -1:] - cumulative), 0.0)
    causal = (positions[:, None] >= positions[None, :]) & (segment_ids[:, None] == segment_ids[None, :])
    decay_table = jnp.exp(jnp.where(causal[None], cumulative[:, :, None] - cumulative[:, None, :], -1e30))
    return enter_weight, leave_weight, decay_table


def reference(inputs, queries, keys, values, out_grad, log_gate, boundaries):
    block_rows = TOK_DEV
    blocks = N_CTX
    feature_width = HEADS * HEAD

    def sequence_step(weight_total, member):
        tokens_in, query_seq, key_seq, value_seq, grad_seq, decay_seq, bounds = member

        def split_rows(array):
            return array.reshape(blocks, block_rows, HEADS, HEAD)

        query_blk = split_rows(query_seq)
        key_blk = split_rows(key_seq)
        value_blk = split_rows(value_seq)
        grad_blk = split_rows(grad_seq)
        token_blk = tokens_in.reshape(blocks, block_rows, DIM)
        decay_blk = decay_seq.reshape(HEADS, blocks, block_rows).transpose(1, 0, 2)
        block_ids = jnp.arange(blocks, dtype=jnp.int32)

        def local_states(item):
            block_id, log_decay, key_one, value_one, query_one, grad_one = item
            positions = block_id * block_rows + jnp.arange(block_rows, dtype=jnp.int32)
            enter_weight, leave_weight, decay_table = block_tables(log_decay, positions, bounds)
            weighted_keys = rounded(leave_weight.T[:, :, None] * key_one.astype(jnp.float32))
            local_state = jnp.einsum('shd,she->hde', weighted_keys, value_one.astype(jnp.float32))
            weighted_queries = rounded(enter_weight.T[:, :, None] * query_one.astype(jnp.float32))
            back_state = jnp.einsum('thd,the->hde', weighted_queries, grad_one.astype(jnp.float32))
            return enter_weight[:, -1], local_state, back_state

        through, local_state, back_state = lax.map(local_states, (block_ids, decay_blk, key_blk, value_blk, query_blk, grad_blk))

        def carry_step(state, item):
            decay_multiplier, term = item
            return rounded(decay_multiplier)[:, None, None] * state + rounded(term), rounded(state)

        zero_state = jnp.zeros((HEADS, HEAD, HEAD), jnp.float32)
        last_state, carried_in = lax.scan(carry_step, zero_state, (through, local_state))
        first_state, carried_back = lax.scan(carry_step, zero_state, (through, back_state), reverse=True)

        def gradient_step(weight_sum, item):
            block_id, log_decay, query_one, key_one, value_one, grad_one, token_one, state_in, state_back = item
            positions = block_id * block_rows + jnp.arange(block_rows, dtype=jnp.int32)
            enter_weight, leave_weight, decay_table = block_tables(log_decay, positions, bounds)
            query_f = query_one.astype(jnp.float32)
            key_f = key_one.astype(jnp.float32)
            value_f = value_one.astype(jnp.float32)
            grad_f = grad_one.astype(jnp.float32)
            score_grad = rounded(decay_table * jnp.einsum('thd,shd->hts', grad_f, value_f))
            score_keys = rounded(decay_table * jnp.einsum('thd,shd->hts', query_f, key_f))
            query_new = jnp.einsum('hts,shd->thd', score_grad, key_f) + enter_weight.T[:, :, None] * jnp.einsum('the,hde->thd', grad_f, state_in)
            key_new = jnp.einsum('hts,thd->shd', score_grad, query_f) + leave_weight.T[:, :, None] * jnp.einsum('she,hde->shd', value_f, state_back)
            value_new = jnp.einsum('hts,thd->shd', score_keys, grad_f) + leave_weight.T[:, :, None] * jnp.einsum('shd,hde->she', key_f, state_back)
            value_grad = value_new.astype(jnp.bfloat16).reshape(block_rows, feature_width)
            block_term = jnp.dot(token_one.T, value_grad, preferred_element_type=jnp.float32)
            weight_sum = weight_sum + rounded(block_term)
            return weight_sum, (query_new.astype(jnp.bfloat16).reshape(block_rows, feature_width), key_new.astype(jnp.bfloat16).reshape(block_rows, feature_width))

        weight_total, grads = lax.scan(gradient_step, weight_total, (block_ids, decay_blk, query_blk, key_blk, value_blk, grad_blk, token_blk, carried_in, carried_back))
        return weight_total, (grads[0].reshape(SEQUENCE_LENGTH, feature_width), grads[1].reshape(SEQUENCE_LENGTH, feature_width))

    weight_start = jnp.zeros((DIM, feature_width), jnp.float32)
    weight_total, grads = lax.scan(sequence_step, weight_start, (inputs, queries, keys, values, out_grad, log_gate, boundaries))
    return grads[0], grads[1], weight_total
```

```python
import functools

import jax
import jax.numpy as jnp
from jax import lax
from jax.experimental import pallas as pl
from jax.experimental.pallas import tpu as pltpu
from jax.sharding import Mesh
from jax.sharding import PartitionSpec as P

F32, BF16 = jnp.float32, jnp.bfloat16
HEAD = 128
TOK = 128
PAIR = 2 * TOK
LINE = 8
SPAN = 4
OWN = 16
PART = OWN // SPAN
STATE = PART * HEAD
TAIL = 16
PLANE = ("y", "x")
CTX = ("y", "x", "core")
VMEM_LIMIT = 16 << 20


def mm(a, b, lhs, rhs):
    return lax.dot_general(a, b, (((lhs,), (rhs,)), ((), ())), preferred_element_type=F32)


def segment_of(bounds_ref, positions):
    total = jnp.zeros_like(positions)
    for j in range(bounds_ref.shape[0]):
        total = total + (bounds_ref[j] <= positions).astype(jnp.int32)
    return total


def scalar_segment(bounds_ref, position):
    total = jnp.int32(0)
    for j in range(bounds_ref.shape[0]):
        total = total + (bounds_ref[j] <= position).astype(jnp.int32)
    return total


def enter_columns(cum_t, bounds_ref, begin):
    positions = begin + lax.broadcasted_iota(jnp.int32, cum_t.shape, 0)
    same = segment_of(bounds_ref, positions) == scalar_segment(bounds_ref, begin - 1)
    return jnp.where(same, jnp.exp(cum_t), 0.0)


def leave_columns(cum_t, bounds_ref, begin):
    positions = begin + lax.broadcasted_iota(jnp.int32, cum_t.shape, 0)
    same = segment_of(bounds_ref, positions) == scalar_segment(bounds_ref, begin + PAIR - 1)
    return jnp.where(same, jnp.exp(cum_t[PAIR - 1 :, :] - cum_t), 0.0)


def head_cut(h):
    return slice(h * HEAD, (h + 1) * HEAD)


def pick(core, source, keep_ref, send_ref):
    for d in range(LINE):
        for target, who in ((keep_ref, core), (send_ref, 1 - core)):
            lanes = pl.ds(pl.multiple_of((2 * d + who) * 2 * HEAD, 2 * HEAD), 2 * HEAD)
            target[:, 2 * d * HEAD : 2 * (d + 1) * HEAD] = source[:, lanes]


def pick_kernel(place_ref, a_ref, b_ref, a_keep, a_send, b_keep, b_send):
    core = place_ref[1]
    pick(core, a_ref, a_keep, a_send)
    pick(core, b_ref, b_keep, b_send)


def pick_gate_kernel(place_ref, gate_ref, *refs):
    core = place_ref[1]
    a_ref, b_ref, gate_keep, gate_send, a_keep, a_send, b_keep, b_send = refs
    for d in range(LINE):
        gate_keep[2 * d : 2 * d + 2, :] = gate_ref[2 * d + core]
        gate_send[2 * d : 2 * d + 2, :] = gate_ref[2 * d + 1 - core]
    pick(core, a_ref, a_keep, a_send)
    pick(core, b_ref, b_keep, b_send)


def turn_kernel(place_ref, x_ref, keep_ref, send_ref, hold):
    core = place_ref[1]
    for j in range(x_ref.shape[1] // TOK):
        hold[j * TOK : (j + 1) * TOK, :] = x_ref[:, j * TOK : (j + 1) * TOK].T
    count, near, _ = keep_ref.shape
    for j in range(count):
        for target, who in ((keep_ref, core), (send_ref, 1 - core)):
            rows = pl.ds(pl.multiple_of((2 * j + who) * near, 16), near)
            target[j] = hold[rows, :]


def pair_kernel(place_ref, keep_ref, other_ref, out_ref):
    first = place_ref[1] == 0
    out_ref[:, :TOK] = jnp.where(first, keep_ref[...], other_ref[...])
    out_ref[:, TOK:] = jnp.where(first, other_ref[...], keep_ref[...])


def join(core, keep_ref, other_ref, out_ref):
    out_ref[pl.ds(pl.multiple_of(core * TOK, TOK), TOK), :] = keep_ref[...]
    out_ref[pl.ds(pl.multiple_of((1 - core) * TOK, TOK), TOK), :] = other_ref[...]


def back_states_kernel(place_ref, bounds_ref, *refs):
    gate_keep, gate_other, q_keep, q_other, g_keep, g_other = refs[:6]
    out_refs, (cum_ref, q_ref, g_ref, hold) = refs[6 : 6 + SPAN], refs[6 + SPAN :]
    begin, core = place_ref[0], place_ref[1]
    join(core, q_keep, q_other, q_ref)
    join(core, g_keep, g_other, g_ref)
    gates = (gate_keep[...], gate_other[...])
    swap = core == 1
    gate = jnp.concatenate(
        [jnp.where(swap, gates[1], gates[0]), jnp.where(swap, gates[0], gates[1])], axis=1
    )
    before = lax.broadcasted_iota(jnp.int32, (PAIR, PAIR), 0)
    after = lax.broadcasted_iota(jnp.int32, (PAIR, PAIR), 1)
    cum = jnp.dot(
        gate,
        (before <= after).astype(F32),
        precision=lax.Precision.HIGHEST,
        preferred_element_type=F32,
    )
    for d in range(LINE):
        cum_ref[d] = cum[2 * d : 2 * d + 2, :]
    enter = enter_columns(cum.T, bounds_ref, begin)
    rows = lax.broadcasted_iota(jnp.int32, (TAIL, HEAD), 0)

    for o in range(SPAN):
        tail = jnp.zeros((TAIL, HEAD), F32)
        for j in range(PART):
            h = o * PART + j
            weighted = (enter[:, h : h + 1] * q_ref[:, head_cut(h)].astype(F32)).astype(BF16)
            hold[o, head_cut(j), :] = mm(weighted, g_ref[:, head_cut(h)], 0, 0).astype(BF16)
            tail = jnp.where(rows == j, enter[PAIR - 1 :, h : h + 1], tail)
        hold[o, STATE:, :] = tail.astype(BF16)
    send_apart(place_ref[3], hold, out_refs)


def columns_of(cum_ref):
    return jnp.concatenate([cum_ref[d] for d in range(cum_ref.shape[0])], axis=0).T


def send_apart(place, hold, out_refs):
    for step, out_ref in enumerate(out_refs):
        out_ref[...] = hold[lax.rem(place + step, len(out_refs))]


def join_kernel(place_ref, a_keep, a_other, b_keep, b_other, a_ref, b_ref):
    join(place_ref[1], a_keep, a_other, a_ref)
    join(place_ref[1], b_keep, b_other, b_ref)


def front_states_kernel(place_ref, bounds_ref, cum_ref, k_ref, v_ref, *refs):
    leave = leave_columns(columns_of(cum_ref), bounds_ref, place_ref[0])

    out_refs, hold = refs[:SPAN], refs[SPAN]
    for o in range(SPAN):
        for j in range(PART):
            h = o * PART + j
            weighted = (leave[:, h : h + 1] * k_ref[:, head_cut(h)].astype(F32)).astype(BF16)
            hold[o, head_cut(j), :] = mm(weighted, v_ref[:, head_cut(h)], 0, 0).astype(BF16)
    send_apart(place_ref[3], hold, out_refs)


def advance(state, part_ref, tail_ref, block):
    pieces = []
    for j in range(PART):
        through = tail_ref[block, j : j + 1, :].astype(F32)
        pieces.append(through * state[head_cut(j)] + part_ref[block, head_cut(j), :].astype(F32))
    return jnp.concatenate(pieces, axis=0)


def walk(backward):
    return reversed(range(SPAN)) if backward else range(SPAN)


def total_kernel(backward, place_ref, *refs):
    parts = refs[:SPAN]
    total_ref, sorted_ref = refs[-3:-1] if backward else refs[-2:]
    tail_ref = refs[-1] if backward else refs[SPAN]
    for step, part in enumerate(parts):
        block = lax.rem(place_ref[3] - step + SPAN, SPAN)
        sorted_ref[block] = part[:STATE, :]
        if backward:
            tail_ref[block] = part[STATE:, :]
    state = jnp.zeros((STATE, HEAD), F32)
    for block in walk(backward):
        state = advance(state, sorted_ref, tail_ref, block)
    total_ref[...] = state.astype(BF16)


def carry_kernel(backward, place_ref, sorted_ref, tail_ref, entry_ref, *refs):
    out_refs, hold = refs[-SPAN - 1 : -1], refs[-1]
    state = entry_ref[...].astype(F32)
    for block in walk(backward):
        hold[block] = state.astype(BF16)
        state = advance(state, sorted_ref, tail_ref, block)
    send_apart(place_ref[3], hold, out_refs)


def take_in(lane, parts, hold):
    for step, part in enumerate(parts):
        hold[lax.rem(lane - step + SPAN, SPAN)] = part[...]


def inner_kernel(i, place_ref, bounds_ref, cum_ref, *refs):
    q_ref, k_ref, v_ref, g_ref = refs[:4]
    query_ref, key_ref, value_ref = refs[-3:]
    begin = place_ref[0]
    cum = cum_ref[...]
    cum_t = cum.T
    row = lax.broadcasted_iota(jnp.int32, (PAIR, PAIR), 0)
    column = lax.broadcasted_iota(jnp.int32, (PAIR, PAIR), 1)
    row_ids = segment_of(bounds_ref, begin + lax.broadcasted_iota(jnp.int32, (PAIR, 1), 0))
    column_ids = segment_of(bounds_ref, begin + lax.broadcasted_iota(jnp.int32, (1, PAIR), 1))
    causal = (row >= column) & (row_ids == column_ids)
    decay = jnp.exp(jnp.where(causal, cum_t[:, i : i + 1] - cum[i : i + 1, :], -1e30))
    q, k, v, g = q_ref[...], k_ref[...], v_ref[...], g_ref[...]
    score_grad = (decay * mm(g, v, 1, 1)).astype(BF16)
    score_keys = (decay * mm(q, k, 1, 1)).astype(BF16)
    query_ref[...] = mm(score_grad, k, 1, 0)
    key_ref[...] = mm(score_grad, q, 0, 0)
    value_ref[...] = mm(score_keys, g, 0, 0)


def value_kernel(place_ref, bounds_ref, cum_ref, k_ref, first_in, second_in, *refs):
    states, out_refs, (hold, out_hold) = refs[:SPAN], refs[-LINE - 2 : -2], refs[-2:]
    take_in(place_ref[3], states, hold)
    leave = leave_columns(columns_of(cum_ref), bounds_ref, place_ref[0])
    for h in range(OWN):
        value_in = (first_in, second_in)[h % 2][:, head_cut(h // 2)]
        state = hold[h // PART, head_cut(h % PART), :]
        extra = leave[:, h : h + 1] * mm(k_ref[:, head_cut(h)], state, 1, 0)
        out_hold[h // 2, :, head_cut(h % 2)] = (value_in + extra).astype(BF16)
    send_apart(place_ref[2], out_hold, out_refs)


def part_rows(core, value, cut, keep_ref, send_ref):
    keep_ref[:, cut] = jnp.where(core == 0, value[:TOK], value[TOK:]).astype(BF16)
    send_ref[:, cut] = jnp.where(core == 0, value[TOK:], value[:TOK]).astype(BF16)


def key_kernel(place_ref, bounds_ref, cum_ref, v_ref, first_in, second_in, *refs):
    states, (keep_ref, send_ref, hold) = refs[:SPAN], refs[-3:]
    take_in(place_ref[3], states, hold)
    leave = leave_columns(columns_of(cum_ref), bounds_ref, place_ref[0])
    for h in range(OWN):
        key_in = (first_in, second_in)[h % 2][:, head_cut(h // 2)]
        state = hold[h // PART, head_cut(h % PART), :]
        extra = leave[:, h : h + 1] * mm(v_ref[:, head_cut(h)], state, 1, 1)
        part_rows(place_ref[1], key_in + extra, head_cut(h), keep_ref, send_ref)


def query_kernel(place_ref, bounds_ref, cum_ref, g_ref, first_in, second_in, *refs):
    states, (keep_ref, send_ref, hold) = refs[:SPAN], refs[-3:]
    take_in(place_ref[3], states, hold)
    enter = enter_columns(columns_of(cum_ref), bounds_ref, place_ref[0])
    for h in range(OWN):
        query_in = (first_in, second_in)[h % 2][:, head_cut(h // 2)]
        state = hold[h // PART, head_cut(h % PART), :]
        extra = enter[:, h : h + 1] * mm(g_ref[:, head_cut(h)], state, 1, 1)
        part_rows(place_ref[1], query_in + extra, head_cut(h), keep_ref, send_ref)


def lay_kernel(place_ref, keep_ref, other_ref, out_ref):
    core = place_ref[1]
    for d in range(LINE):
        near = slice(2 * d * HEAD, 2 * (d + 1) * HEAD)
        for source, who in ((keep_ref, core), (other_ref, 1 - core)):
            lanes = pl.ds(pl.multiple_of((2 * d + who) * 2 * HEAD, 2 * HEAD), 2 * HEAD)
            out_ref[:, lanes] = source[:, near]


def weight_kernel(place_ref, *refs):
    rows, keeps, others = (refs[n * LINE : (n + 1) * LINE] for n in range(3))
    out_ref, core = refs[-1], place_ref[1]
    right = []
    for keep, other in zip(keeps, others, strict=True):
        a, b = keep[...], other[...]
        right.append(
            jnp.concatenate([jnp.where(core == 0, a, b), jnp.where(core == 0, b, a)], axis=1)
        )
    near = out_ref.shape[1]
    tall = SPAN * near
    for j in range(out_ref.shape[0] // SPAN):
        cut = slice(j * tall, (j + 1) * tall)
        acc = mm(rows[0][cut, :], right[0], 1, 0)
        for n in range(1, LINE):
            acc = acc + mm(rows[n][cut, :], right[n], 1, 0)
        acc = acc.astype(BF16)
        for i in range(SPAN):
            out_ref[j * SPAN + i] = acc[i * near : (i + 1) * near]


def sum_kernel(parts_ref, out_ref):
    total = parts_ref[0].astype(F32)
    for j in range(1, parts_ref.shape[0]):
        total = total + parts_ref[j].astype(F32)
    out_ref[...] = total


def shape(dims, dtype=BF16):
    return jax.ShapeDtypeStruct(dims, dtype)


def cost():
    return pl.CostEstimate(flops=1, bytes_accessed=1, transcendentals=0)


def held(values, after):
    spec = pl.BlockSpec(memory_space=pl.ANY)
    return pl.pallas_call(
        lambda *refs: None,
        in_specs=[spec] * (len(values) + len(after)),
        out_specs=[spec] * len(values),
        out_shape=[shape(v.shape, v.dtype) for v in values],
        input_output_aliases={n: n for n in range(len(values))},
        compiler_params=pltpu.CompilerParams(vmem_limit_bytes=VMEM_LIMIT),
        cost_estimate=cost(),
    )(*values, *after)


def whole(kernel, smem, arrays, outs, scratch=(), after=()):
    vmem = pl.BlockSpec(memory_space=pltpu.VMEM)
    count = len(smem) + len(arrays)

    def body(*refs):
        kernel(*refs[:count], *refs[count + len(after) :])

    return pl.pallas_call(
        body,
        in_specs=[pl.BlockSpec(memory_space=pltpu.SMEM)] * len(smem)
        + [vmem] * len(arrays)
        + [pl.BlockSpec(memory_space=pl.ANY)] * len(after),
        out_specs=[vmem] * len(outs),
        out_shape=outs,
        scratch_shapes=list(scratch),
        compiler_params=pltpu.CompilerParams(vmem_limit_bytes=VMEM_LIMIT),
        cost_estimate=cost(),
    )(*smem, *arrays, *after)


def inner(i, smem, cum, arrays, after):
    outs = [shape((PAIR, LINE * HEAD), F32)] * 3
    return pl.pallas_call(
        functools.partial(inner_kernel, i),
        grid=(LINE,),
        in_specs=[pl.BlockSpec(memory_space=pltpu.SMEM)] * len(smem)
        + [pl.BlockSpec((None, 2, PAIR), lambda d: (d, 0, 0))]
        + [pl.BlockSpec((PAIR, HEAD), lambda d: (0, 2 * d + i))] * len(arrays)
        + [pl.BlockSpec(memory_space=pl.ANY)] * len(after),
        out_specs=[pl.BlockSpec((PAIR, HEAD), lambda d: (0, d))] * len(outs),
        out_shape=outs,
        compiler_params=pltpu.CompilerParams(vmem_limit_bytes=VMEM_LIMIT),
        cost_estimate=cost(),
    )(*smem, cum, *arrays, *after)


def shifted(value, axis, step):
    count = lax.axis_size(axis)
    return lax.ppermute(value, axis, [(i, (i + step) % count) for i in range(count)])


def swapped(value):
    return shifted(value, "core", 1)


def exchange(pieces, axis):
    return [pieces[0]] + [shifted(pieces[s], axis, s) for s in range(1, len(pieces))]


def per_device(inputs, queries, keys, values, out_grad, log_gate, boundaries):
    q, k, v, g = queries[0], keys[0], values[0], out_grad[0]
    width = q.shape[1]
    model = inputs.shape[2]
    core, x, y = lax.axis_index("core"), lax.axis_index("x"), lax.axis_index("y")
    begin = (y * lax.axis_size("x") + x) * PAIR
    place = jnp.stack([begin, core, lax.axis_index("z"), x, y]).astype(jnp.int32)
    smem = (place, boundaries[0])
    plane = lax.axis_size("y") * lax.axis_size("x")
    count = lax.axis_size("y")
    half, chip = shape((TOK, width // 2)), shape((PAIR, width // 2))
    gate_half, cums = shape((OWN, TOK), F32), shape((LINE, 2, PAIR), F32)
    state, states, tails = shape((STATE, HEAD)), shape((SPAN, STATE, HEAD)), shape((SPAN, TAIL, HEAD))
    hold_states = pltpu.VMEM((SPAN, STATE, HEAD), BF16)

    line = shape((plane, model // plane // 2, TOK))
    a_keep, a_send = whole(
        turn_kernel, (place,), [inputs[0]], [line] * 2, [pltpu.VMEM((model, TOK), BF16)]
    )
    a_other = swapped(a_send)
    (own,) = whole(
        pair_kernel,
        (place,),
        [a.reshape(model // 2, TOK) for a in (a_keep, a_other)],
        [shape((model // 2, PAIR))],
    )
    right_1, left_1 = shifted(own, "z", 1), shifted(own, "z", -1)
    gate_keep, gate_send, q_keep, q_send, g_keep, g_send = whole(
        pick_gate_kernel,
        (place,),
        [log_gate[0].reshape(OWN, 2, TOK), q, g],
        [gate_half] * 2 + [half] * 4,
        after=[own],
    )
    gate_other, q_other, g_other = swapped(gate_send), swapped(q_send), swapped(g_send)
    k_keep, k_send, v_keep, v_send = whole(
        pick_kernel, (place,), [k, v], [half] * 4, after=[q_send]
    )
    k_other, v_other = swapped(k_send), swapped(v_send)
    *back, cum, q, g = whole(
        back_states_kernel,
        smem,
        [gate_keep, gate_other, q_keep, q_other, g_keep, g_other],
        [shape((STATE + TAIL, HEAD))] * SPAN + [cums, chip, chip],
        [pltpu.VMEM((SPAN, STATE + TAIL, HEAD), BF16)],
        after=[k_send],
    )
    started = back[0]
    back = exchange(back, "x")
    k, v = whole(
        join_kernel, (place,), [k_keep, k_other, v_keep, v_other], [chip, chip], after=[started]
    )
    first_in = inner(0, smem, cum, [q, k, v, g], [])
    right_1, left_1 = held([right_1, left_1], [first_in[0]])
    right_2, left_2 = shifted(right_1, "z", 1), shifted(left_1, "z", -1)
    front = whole(
        front_states_kernel, smem, [cum, k, v], [state] * SPAN, [hold_states], after=[right_1]
    )
    second_in = inner(1, smem, cum, [q, k, v, g], [front[0]])

    back = held(back, [second_in[0]])
    back_total, back, tail = whole(
        functools.partial(total_kernel, True), (place,), back, [state, states, tails]
    )
    back_entry = lax.ppermute(back_total, "y", [(i + 1, i) for i in range(count - 1)])
    (carried_back) = whole(
        functools.partial(carry_kernel, True),
        (place,),
        [back, tail, back_entry],
        [state] * SPAN,
        [hold_states],
    )
    front = held(front, [carried_back[0]])
    carried_back = exchange(carried_back, "x")
    front = exchange(front, "x")
    right_2, left_2 = held([right_2, left_2], [carried_back[1]])
    right_3, left_3 = shifted(right_2, "z", 1), shifted(left_2, "z", -1)
    columns = whole(
        value_kernel,
        smem,
        [cum, k, first_in[2], second_in[2], *carried_back],
        [shape((PAIR, 2 * HEAD))] * LINE,
        [hold_states, pltpu.VMEM((LINE, PAIR, 2 * HEAD), BF16)],
        after=[right_2],
    )
    started = columns[0]
    columns = exchange(columns, "z")
    front = held(front, [started])
    front_total, front = whole(
        functools.partial(total_kernel, False), (place,), [*front, tail], [state, states]
    )
    front_entry = lax.ppermute(front_total, "y", [(i, i + 1) for i in range(count - 1)])
    carried_in = whole(
        functools.partial(carry_kernel, False),
        (place,),
        [front, tail, front_entry],
        [state] * SPAN,
        [hold_states],
    )
    started = carried_in[0]
    carried_in = exchange(carried_in, "x")
    right_3, left_3 = held([right_3, left_3], [started])
    left_4 = shifted(left_3, "z", -1)
    key_keep, key_send = whole(
        key_kernel,
        smem,
        [cum, v, first_in[1], second_in[1], *carried_back],
        [half] * 2,
        [hold_states],
        after=[right_3],
    )
    key_other = swapped(key_send)
    query_keep, query_send = whole(
        query_kernel,
        smem,
        [cum, g, first_in[0], second_in[0], *carried_in],
        [half] * 2,
        [hold_states],
        after=[key_send],
    )
    query_other = swapped(query_send)
    order = [0, 1, LINE - 1, 2, LINE - 2, 3, LINE - 3, 4]
    near = model // plane // 2
    columns = [columns[n] for n in order]
    (partial,) = whole(
        weight_kernel,
        (place,),
        [own, right_1, left_1, right_2, left_2, right_3, left_3, left_4]
        + [*columns, *map(swapped, columns)],
        [shape((plane, near, 4 * HEAD))],
        after=[query_send],
    )
    (key_grad,) = whole(
        lay_kernel, (place,), [key_keep, key_other], [shape((TOK, width))], after=[partial]
    )
    (query_grad,) = whole(
        lay_kernel, (place,), [query_keep, query_other], [shape((TOK, width))], after=[partial]
    )
    parts = lax.all_to_all(partial, PLANE, 0, 0)
    (weight,) = whole(sum_kernel, (), [parts], [shape((near, 4 * HEAD), F32)])
    return query_grad[None], key_grad[None], weight


def solution(mesh):
    fine = Mesh(mesh.devices.reshape(LINE, 4, SPAN, 2), ("z", "y", "x", "core"))
    rows = P("z", CTX, None)
    in_specs = (rows, rows, rows, rows, rows, P("z", None, CTX), P("z", None))
    out_specs = (rows, rows, P(CTX, "z"))
    return jax.shard_map(
        per_device, mesh=fine, in_specs=in_specs, out_specs=out_specs, check_vma=False
    )
```

```python
import functools
import itertools

import jax
import jax.numpy as jnp
from jax import lax
from jax.experimental import pallas as pl
from jax.experimental.pallas import tpu as pltpu
from jax.sharding import Mesh
from jax.sharding import PartitionSpec as P

F32, BF16 = jnp.float32, jnp.bfloat16
HEAD = 128
TOK = 128
PAIR = 2 * TOK
LINE = 8
SPAN = 4
OWN = 16
PART = OWN // SPAN
STATE = PART * HEAD
TAIL = 16
CTX = ("y", "x", "core")
VMEM_LIMIT = 16 << 20
HEAVY = 33
WEIGHTS = (33, 33, 31)
CUTS = (0, 3, 6, 8)


def mm(a, b, lhs, rhs):
    return lax.dot_general(a, b, (((lhs,), (rhs,)), ((), ())), preferred_element_type=F32)


def segment_of(bounds_ref, positions):
    total = jnp.zeros_like(positions)
    for j in range(bounds_ref.shape[0]):
        total = total + (bounds_ref[j] <= positions).astype(jnp.int32)
    return total


def scalar_segment(bounds_ref, position):
    total = jnp.int32(0)
    for j in range(bounds_ref.shape[0]):
        total = total + (bounds_ref[j] <= position).astype(jnp.int32)
    return total


def enter_columns(cum_t, bounds_ref, begin):
    positions = begin + lax.broadcasted_iota(jnp.int32, cum_t.shape, 0)
    same = segment_of(bounds_ref, positions) == scalar_segment(bounds_ref, begin - 1)
    return jnp.where(same, jnp.exp(cum_t), 0.0)


def leave_columns(cum_t, bounds_ref, begin):
    positions = begin + lax.broadcasted_iota(jnp.int32, cum_t.shape, 0)
    same = segment_of(bounds_ref, positions) == scalar_segment(bounds_ref, begin + PAIR - 1)
    return jnp.where(same, jnp.exp(cum_t[PAIR - 1 :, :] - cum_t), 0.0)


def head_cut(h):
    return slice(h * HEAD, (h + 1) * HEAD)


def pick_kernel(place_ref, gate_ref, *refs):
    core = place_ref[1]
    sources, (gate_keep, gate_send, keep_ref, send_ref) = refs[:4], refs[4:]
    for d in range(LINE):
        gate_keep[2 * d : 2 * d + 2, :] = gate_ref[2 * d + core]
        gate_send[2 * d : 2 * d + 2, :] = gate_ref[2 * d + 1 - core]
        for target, who in ((keep_ref, core), (send_ref, 1 - core)):
            lanes = pl.ds(pl.multiple_of((2 * d + who) * 2 * HEAD, 2 * HEAD), 2 * HEAD)
            for n, source in enumerate(sources):
                target[n, :, 2 * d * HEAD : 2 * (d + 1) * HEAD] = source[:, lanes]


def turn_kernel(place_ref, x_ref, keep_ref, send_ref, hold):
    core = place_ref[1]
    for j in range(x_ref.shape[1] // TOK):
        hold[j * TOK : (j + 1) * TOK, :] = x_ref[:, j * TOK : (j + 1) * TOK].T
    count, near, _ = keep_ref.shape
    for j in range(count):
        for target, who in ((keep_ref, core), (send_ref, 1 - core)):
            rows = pl.ds(pl.multiple_of((2 * j + who) * near, 16), near)
            target[j] = hold[rows, :]


def pair_kernel(place_ref, keep_ref, other_ref, out_ref):
    first = place_ref[1] == 0
    out_ref[:, :TOK] = jnp.where(first, keep_ref[...], other_ref[...])
    out_ref[:, TOK:] = jnp.where(first, other_ref[...], keep_ref[...])


def join(core, n, keep_ref, other_ref, out_ref):
    out_ref[pl.ds(pl.multiple_of(core * TOK, TOK), TOK), :] = keep_ref[n]
    out_ref[pl.ds(pl.multiple_of((1 - core) * TOK, TOK), TOK), :] = other_ref[n]


def states_kernel(place_ref, bounds_ref, *refs):
    gate_keep, gate_other, keep_ref, other_ref = refs[:4]
    out_refs, refs = refs[4 : 4 + SPAN], refs[4 + SPAN :]
    cum_ref, q_ref, g_ref, k_ref, v_ref, hold = refs
    begin, core = place_ref[0], place_ref[1]
    for n, ref in enumerate((q_ref, g_ref, k_ref, v_ref)):
        join(core, n, keep_ref, other_ref, ref)
    gates = (gate_keep[...], gate_other[...])
    swap = core == 1
    gate = jnp.concatenate(
        [jnp.where(swap, gates[1], gates[0]), jnp.where(swap, gates[0], gates[1])], axis=1
    )
    before = lax.broadcasted_iota(jnp.int32, (PAIR, PAIR), 0)
    after = lax.broadcasted_iota(jnp.int32, (PAIR, PAIR), 1)
    cum = jnp.dot(
        gate,
        (before <= after).astype(F32),
        precision=lax.Precision.HIGHEST,
        preferred_element_type=F32,
    )
    for d in range(LINE):
        cum_ref[d] = cum[2 * d : 2 * d + 2, :]
    enter = enter_columns(cum.T, bounds_ref, begin)
    leave = leave_columns(cum.T, bounds_ref, begin)
    rows = lax.broadcasted_iota(jnp.int32, (TAIL, HEAD), 0)
    for o in range(SPAN):
        tail = jnp.zeros((TAIL, HEAD), F32)
        for j in range(PART):
            h = o * PART + j
            weighted = (enter[:, h : h + 1] * q_ref[:, head_cut(h)].astype(F32)).astype(BF16)
            hold[o, head_cut(j), :] = mm(weighted, g_ref[:, head_cut(h)], 0, 0).astype(BF16)
            weighted = (leave[:, h : h + 1] * k_ref[:, head_cut(h)].astype(F32)).astype(BF16)
            hold[o, head_cut(PART + j), :] = mm(weighted, v_ref[:, head_cut(h)], 0, 0).astype(BF16)
            tail = jnp.where(rows == j, enter[PAIR - 1 :, h : h + 1], tail)
        hold[o, 2 * STATE :, :] = tail.astype(BF16)
    send_apart(place_ref[3], hold, out_refs)


def columns_of(cum_ref):
    return jnp.concatenate([cum_ref[d] for d in range(cum_ref.shape[0])], axis=0).T


def send_apart(place, hold, out_refs):
    for step, out_ref in enumerate(out_refs):
        out_ref[...] = hold[lax.rem(place + step, len(out_refs))]


def advance(state, hold, block, backward):
    pieces = []
    for j in range(PART):
        through = hold[block, 2 * STATE + j : 2 * STATE + j + 1, :].astype(F32)
        part = hold[block, head_cut(j if backward else PART + j), :].astype(F32)
        pieces.append(through * state[head_cut(j)] + part)
    return jnp.concatenate(pieces, axis=0)


def walk(backward):
    return reversed(range(SPAN)) if backward else range(SPAN)


def total_kernel(place_ref, *refs):
    parts, (back_ref, front_ref, sorted_ref) = refs[:SPAN], refs[SPAN:]
    take_in(place_ref[3], parts, sorted_ref)
    for backward, total_ref in ((True, back_ref), (False, front_ref)):
        state = jnp.zeros((STATE, HEAD), F32)
        for block in walk(backward):
            state = advance(state, sorted_ref, block, backward)
        total_ref[...] = state.astype(BF16)


def carry_kernel(place_ref, sorted_ref, back_ref, front_ref, *refs):
    out_refs, hold = refs[:SPAN], refs[SPAN]
    for backward, entry_ref in ((True, back_ref), (False, front_ref)):
        state = entry_ref[...].astype(F32)
        cut = slice(0, STATE) if backward else slice(STATE, 2 * STATE)
        for block in walk(backward):
            hold[block, cut, :] = state.astype(BF16)
            state = advance(state, sorted_ref, block, backward)
    send_apart(place_ref[3], hold, out_refs)


def take_in(lane, parts, hold):
    for step, part in enumerate(parts):
        hold[lax.rem(lane - step + SPAN, SPAN)] = part[...]


def inner_kernel(place_ref, bounds_ref, cum_ref, *refs):
    q_ref, k_ref, v_ref, g_ref, query_ref, key_ref, value_ref = refs
    begin = place_ref[0]
    cum = cum_ref[...]
    cum_t = cum.T
    row = lax.broadcasted_iota(jnp.int32, (PAIR, PAIR), 0)
    column = lax.broadcasted_iota(jnp.int32, (PAIR, PAIR), 1)
    row_ids = segment_of(bounds_ref, begin + lax.broadcasted_iota(jnp.int32, (PAIR, 1), 0))
    column_ids = segment_of(bounds_ref, begin + lax.broadcasted_iota(jnp.int32, (1, PAIR), 1))
    causal = (row >= column) & (row_ids == column_ids)
    for h in range(cum.shape[0]):
        cut = head_cut(h)
        decay = jnp.exp(jnp.where(causal, cum_t[:, h : h + 1] - cum[h : h + 1, :], -1e30))
        q, k, v, g = q_ref[:, cut], k_ref[:, cut], v_ref[:, cut], g_ref[:, cut]
        score_grad = (decay * mm(g, v, 1, 1)).astype(BF16)
        score_keys = (decay * mm(q, k, 1, 1)).astype(BF16)
        query_ref[:, cut] = mm(score_grad, k, 1, 0)
        key_ref[:, cut] = mm(score_grad, q, 0, 0)
        value_ref[:, cut] = mm(score_keys, g, 0, 0)


def piece_of(parts, h):
    for low, high, part in zip(CUTS, CUTS[1:], parts):
        if low <= h // 2 < high:
            return part[:, head_cut(h - 2 * low)]


def value_kernel(place_ref, bounds_ref, cum_ref, k_ref, *refs):
    value_in, states, refs = refs[:3], refs[3 : 3 + SPAN], refs[3 + SPAN :]
    far_ref, send_ref, keep_ref, hold, out_hold = refs
    core, deep = place_ref[1], place_ref[2]
    take_in(place_ref[3], states, hold)
    leave = leave_columns(columns_of(cum_ref), bounds_ref, place_ref[0])
    for h in range(OWN):
        state = hold[h // PART, head_cut(h % PART), :]
        extra = leave[:, h : h + 1] * mm(k_ref[:, head_cut(h)], state, 1, 0)
        out_hold[h // 2, :, head_cut(h % 2)] = (piece_of(value_in, h) + extra).astype(BF16)
    keep_ref[LINE // 2 - 1] = out_hold[deep]
    send_ref[LINE // 2 - 1] = out_hold[deep]
    far_ref[...] = out_hold[lax.rem(deep + LINE // 2, LINE)]
    for n in range(LINE // 2 - 1):
        ahead, behind = lax.rem(deep + 1 + n, LINE), lax.rem(deep + LINE - 1 - n, LINE)
        keep_ref[n] = out_hold[jnp.where(core == 0, ahead, behind)]
        send_ref[n] = out_hold[jnp.where(core == 0, behind, ahead)]


def bundle_kernel(keep_ref, other_ref, *out_refs):
    for n, out_ref in enumerate(out_refs):
        out_ref[0] = keep_ref[n]
        out_ref[1] = other_ref[n]


def part_rows(core, value, cut, keep_ref, send_ref):
    keep_ref[:, cut] = jnp.where(core == 0, value[:TOK], value[TOK:]).astype(BF16)
    send_ref[:, cut] = jnp.where(core == 0, value[TOK:], value[:TOK]).astype(BF16)


def key_kernel(place_ref, bounds_ref, cum_ref, v_ref, *refs):
    key_in, states, (keep_ref, send_ref, hold) = refs[:3], refs[3 : 3 + SPAN], refs[3 + SPAN :]
    take_in(place_ref[3], states, hold)
    leave = leave_columns(columns_of(cum_ref), bounds_ref, place_ref[0])
    for h in range(OWN):
        state = hold[h // PART, head_cut(h % PART), :]
        extra = leave[:, h : h + 1] * mm(v_ref[:, head_cut(h)], state, 1, 1)
        part_rows(place_ref[1], piece_of(key_in, h) + extra, head_cut(h), keep_ref, send_ref)


def query_kernel(place_ref, bounds_ref, cum_ref, g_ref, *refs):
    query_in, states, (keep_ref, send_ref, hold) = refs[:3], refs[3 : 3 + SPAN], refs[3 + SPAN :]
    take_in(place_ref[3], states, hold)
    enter = enter_columns(columns_of(cum_ref), bounds_ref, place_ref[0])
    for h in range(OWN):
        state = hold[h // PART, head_cut(PART + h % PART), :]
        extra = enter[:, h : h + 1] * mm(g_ref[:, head_cut(h)], state, 1, 1)
        part_rows(place_ref[1], piece_of(query_in, h) + extra, head_cut(h), keep_ref, send_ref)


def lay_kernel(place_ref, keep_ref, other_ref, out_ref):
    core = place_ref[1]
    for d in range(LINE):
        near = slice(2 * d * HEAD, 2 * (d + 1) * HEAD)
        for source, who in ((keep_ref, core), (other_ref, 1 - core)):
            lanes = pl.ds(pl.multiple_of((2 * d + who) * 2 * HEAD, 2 * HEAD), 2 * HEAD)
            out_ref[:, lanes] = source[:, near]


def weight_kernel(place_ref, *refs):
    rows, refs = refs[:LINE], refs[LINE:]
    own, far, near_refs = refs[0], refs[1:3], refs[3:9]
    out_refs, hold = refs[9 : 9 + SPAN], refs[9 + SPAN]
    core, x, y = place_ref[1], place_ref[3], place_ref[4]
    first = core == 0

    def both(pair):
        a, b = pair
        return jnp.concatenate([jnp.where(first, a, b), jnp.where(first, b, a)], axis=1)

    right = [both((own[0], own[1]))]
    for n in range(LINE // 2 - 1):
        here, there = near_refs[2 * n], near_refs[2 * n + 1]
        before = [jnp.where(first, here[i], there[i]) for i in range(2)]
        after = [jnp.where(first, there[i], here[i]) for i in range(2)]
        right.append(jnp.concatenate(before, axis=1))
        right.append(jnp.concatenate(after[::-1], axis=1))
    right.append(both((far[0][...], far[1][...])))
    near = hold.shape[1]
    tall = SPAN * near
    for j in range(SPAN):
        cut = slice(j * tall, (j + 1) * tall)
        acc = mm(rows[0][cut, :], right[0], 1, 0)
        for n in range(1, LINE):
            acc = acc + mm(rows[n][cut, :], right[n], 1, 0)
        acc = acc.astype(BF16)
        for i in range(SPAN):
            hold[j * SPAN + i] = acc[i * near : (i + 1) * near]
    for step, out_ref in enumerate(out_refs):
        there_x, there_y = lax.rem(x + step, SPAN), lax.rem(y + step, SPAN)
        for n in range(SPAN):
            out_ref[n] = hold[jnp.where(first, n * SPAN + there_x, there_y * SPAN + n)]


def halfway_kernel(place_ref, *refs):
    parts, out_refs, hold = refs[:SPAN], refs[SPAN : 2 * SPAN], refs[2 * SPAN]
    for n in range(SPAN):
        total = parts[0][n].astype(F32)
        for part in parts[1:]:
            total = total + part[n].astype(F32)
        hold[n] = total.astype(BF16)
    send_apart(jnp.where(place_ref[1] == 0, place_ref[4], place_ref[3]), hold, out_refs)


def sum_kernel(*refs):
    parts, out_ref = refs[:-1], refs[-1]
    total = parts[0][...].astype(F32)
    for part in parts[1:]:
        total = total + part[...].astype(F32)
    out_ref[...] = total


def shape(dims, dtype=BF16):
    return jax.ShapeDtypeStruct(dims, dtype)


def cost(heavy=0):
    return pl.CostEstimate(
        flops=1 << heavy, bytes_accessed=1, transcendentals=0
    )


def held(values, after):
    spec = pl.BlockSpec(memory_space=pl.ANY)
    return pl.pallas_call(
        lambda *refs: None,
        in_specs=[spec] * (len(values) + len(after)),
        out_specs=[spec] * len(values),
        out_shape=[shape(v.shape, v.dtype) for v in values],
        input_output_aliases={n: n for n in range(len(values))},
        compiler_params=pltpu.CompilerParams(vmem_limit_bytes=VMEM_LIMIT),
        cost_estimate=cost(),
    )(*values, *after)


def whole(kernel, smem, arrays, outs, scratch=(), after=(), heavy=0):
    vmem = pl.BlockSpec(memory_space=pltpu.VMEM)
    count = len(smem) + len(arrays)

    def body(*refs):
        kernel(*refs[:count], *refs[count + len(after) :])

    return pl.pallas_call(
        body,
        in_specs=[pl.BlockSpec(memory_space=pltpu.SMEM)] * len(smem)
        + [vmem] * len(arrays)
        + [pl.BlockSpec(memory_space=pl.ANY)] * len(after),
        out_specs=[vmem] * len(outs),
        out_shape=outs,
        scratch_shapes=list(scratch),
        compiler_params=pltpu.CompilerParams(vmem_limit_bytes=VMEM_LIMIT),
        cost_estimate=cost(heavy),
    )(*smem, *arrays, *after)


def inner(part, smem, cum, arrays, after):
    low, high = CUTS[part], CUTS[part + 1]
    outs = [shape((PAIR, (high - low) * 2 * HEAD), F32)] * 3
    count = len(smem) + 1 + len(arrays)

    def body(*refs):
        inner_kernel(*refs[:count], *refs[count + len(after) :])

    return pl.pallas_call(
        body,
        grid=(high - low,),
        in_specs=[pl.BlockSpec(memory_space=pltpu.SMEM)] * len(smem)
        + [pl.BlockSpec((None, 2, PAIR), lambda d: (d + low, 0, 0))]
        + [pl.BlockSpec((PAIR, 2 * HEAD), lambda d: (0, d + low))] * len(arrays)
        + [pl.BlockSpec(memory_space=pl.ANY)] * len(after),
        out_specs=[pl.BlockSpec((PAIR, 2 * HEAD), lambda d: (0, d))] * len(outs),
        out_shape=outs,
        compiler_params=pltpu.CompilerParams(vmem_limit_bytes=VMEM_LIMIT),
        cost_estimate=cost(WEIGHTS[part]),
    )(*smem, cum, *arrays, *after)


def shifted(value, axis, step):
    count = lax.axis_size(axis)
    return lax.ppermute(value, axis, [(i, (i + step) % count) for i in range(count)])


def swapped(value):
    return shifted(value, "core", 1)


def exchange(pieces, axis):
    return [pieces[0]] + [shifted(pieces[s], axis, s) for s in range(1, len(pieces))]


def apart(value, axes, moves):
    sizes = [lax.axis_size(a) for a in axes]
    pairs = []
    for place in itertools.product(*map(range, sizes)):
        for core, move in enumerate(moves):
            there = [(p + m) % n for p, m, n in zip(place, move, sizes, strict=True)]
            index = lambda at: functools.reduce(lambda t, pn: t * pn[1] + pn[0], zip(at, sizes), 0)
            pairs.append((2 * index(place) + core, 2 * index(there) + core))
    return lax.ppermute(value, (*axes, "core"), pairs)


def per_device(inputs, queries, keys, values, out_grad, log_gate, boundaries):
    q, k, v, g = queries[0], keys[0], values[0], out_grad[0]
    width = q.shape[1]
    model = inputs.shape[2]
    core, x, y = lax.axis_index("core"), lax.axis_index("x"), lax.axis_index("y")
    begin = (y * lax.axis_size("x") + x) * PAIR
    place = jnp.stack([begin, core, lax.axis_index("z"), x, y]).astype(jnp.int32)
    smem = (place, boundaries[0])
    plane = lax.axis_size("y") * lax.axis_size("x")
    count = lax.axis_size("y")
    half, chip = shape((TOK, width // 2)), shape((PAIR, width // 2))
    gate_half, cums = shape((OWN, TOK), F32), shape((LINE, 2, PAIR), F32)
    state, span = shape((STATE, HEAD)), (SPAN, 2 * STATE + TAIL, HEAD)
    hold_states = pltpu.VMEM((SPAN, 2 * STATE, HEAD), BF16)

    line = shape((plane, model // plane // 2, TOK))
    a_keep, a_send = whole(
        turn_kernel, (place,), [inputs[0]], [line] * 2, [pltpu.VMEM((model, TOK), BF16)]
    )
    a_other = swapped(a_send)
    (own,) = whole(
        pair_kernel,
        (place,),
        [a.reshape(model // 2, TOK) for a in (a_keep, a_other)],
        [shape((model // 2, PAIR))],
    )
    right_1, left_1 = shifted(own, "z", 1), shifted(own, "z", -1)
    gate_keep, gate_send, keep, send = whole(
        pick_kernel,
        (place,),
        [log_gate[0].reshape(OWN, 2, TOK), q, g, k, v],
        [gate_half] * 2 + [shape((4, *half.shape))] * 2,
        after=[own],
        heavy=HEAVY,
    )
    *parts, cum, q, g, k, v = whole(
        states_kernel,
        smem,
        [gate_keep, swapped(gate_send), keep, swapped(send)],
        [shape(span[1:])] * SPAN + [cums] + [chip] * 4,
        [pltpu.VMEM(span, BF16)],
    )
    parts = exchange(parts, "x")
    inner_1 = inner(0, smem, cum, [q, k, v, g], [])
    right_1, left_1 = held([right_1, left_1], [inner_1[0]])
    right_2, left_2 = shifted(right_1, "z", 1), shifted(left_1, "z", -1)
    inner_2 = inner(1, smem, cum, [q, k, v, g], [right_1])
    parts = held(parts, [inner_2[0]])
    back, front, parts = whole(total_kernel, (place,), parts, [state, state, shape(span)])
    back = lax.ppermute(back, "y", [(i + 1, i) for i in range(count - 1)])
    front = lax.ppermute(front, "y", [(i, i + 1) for i in range(count - 1)])
    carried = whole(
        carry_kernel,
        (place,),
        [parts, back, front],
        [shape((2 * STATE, HEAD))] * SPAN,
        [hold_states],
    )
    inner_3 = inner(2, smem, cum, [q, k, v, g], [carried[0]])
    carried = exchange(carried, "x")
    right_2, left_2 = held([right_2, left_2], [inner_3[0]])
    right_3, left_3 = shifted(right_2, "z", 1), shifted(left_2, "z", -1)
    carried = held(carried, [right_2])
    query_in, key_in, value_in = zip(inner_1, inner_2, inner_3)
    several = shape((LINE // 2, PAIR, 2 * HEAD))
    far_part, send, keep = whole(
        value_kernel,
        smem,
        [cum, k, *value_in, *carried],
        [shape((PAIR, 2 * HEAD)), several, several],
        [hold_states, pltpu.VMEM((LINE, PAIR, 2 * HEAD), BF16)],
        heavy=HEAVY,
    )
    *bundles, own_part = whole(
        bundle_kernel, (), [keep, swapped(send)], [shape((2, PAIR, 2 * HEAD))] * (LINE // 2)
    )
    started = bundles[0]
    bundles = [apart(b, ("z",), [(n + 1,), (-n - 1,)]) for n, b in enumerate(bundles)]
    key_keep, key_send = whole(
        key_kernel,
        smem,
        [cum, v, *key_in, *carried],
        [half] * 2,
        [hold_states],
        after=[started],
        heavy=29,
    )
    key_other = swapped(key_send)
    right_3, left_3 = held([right_3, left_3], [key_send])
    left_4 = shifted(left_3, "z", -1)
    (far_part,) = held([far_part], [right_3])
    far_part = apart(far_part, ("z",), [(LINE // 2,), (LINE // 2,)])
    query_keep, query_send = whole(
        query_kernel,
        smem,
        [cum, g, *query_in, *carried],
        [half] * 2,
        [hold_states],
        after=[right_3],
        heavy=29,
    )
    query_other = swapped(query_send)
    near = model // plane // 2
    columns = [own_part, far_part, swapped(far_part)]
    for b in bundles:
        columns += [b, swapped(b)]
    parts = whole(
        weight_kernel,
        (place,),
        [own, right_1, left_1, right_2, left_2, right_3, left_3, left_4, *columns],
        [shape((SPAN, near, 4 * HEAD))] * SPAN,
        [pltpu.VMEM((plane, near, 4 * HEAD), BF16)],
        after=[query_send],
    )
    started = parts[0]
    parts = [parts[0]] + [apart(parts[n], ("y", "x"), [(0, n), (n, 0)]) for n in range(1, SPAN)]
    (key_grad,) = whole(
        lay_kernel, (place,), [key_keep, key_other], [shape((TOK, width))], after=[started], heavy=HEAVY
    )
    parts = held(parts, [key_grad])
    parts = whole(
        halfway_kernel,
        (place,),
        parts,
        [shape((near, 4 * HEAD))] * SPAN,
        [pltpu.VMEM((SPAN, near, 4 * HEAD), BF16)],
    )
    started = parts[0]
    parts = [parts[0]] + [apart(parts[n], ("y", "x"), [(n, 0), (0, n)]) for n in range(1, SPAN)]
    (query_grad,) = whole(
        lay_kernel,
        (place,),
        [query_keep, query_other],
        [shape((TOK, width))],
        after=[started],
        heavy=HEAVY,
    )
    parts = held(parts, [query_grad])
    (weight,) = whole(sum_kernel, (), parts, [shape((near, 4 * HEAD), F32)])
    return query_grad[None], key_grad[None], weight


def solution(mesh):
    fine = Mesh(mesh.devices.reshape(LINE, 4, SPAN, 2), ("z", "y", "x", "core"))
    rows = P("z", CTX, None)
    in_specs = (rows, rows, rows, rows, rows, P("z", None, CTX), P("z", None))
    out_specs = (rows, rows, P(CTX, "z"))
    return jax.shard_map(
        per_device, mesh=fine, in_specs=in_specs, out_specs=out_specs, check_vma=False
    )
```

```python
import functools
import itertools

import jax
import jax.numpy as jnp
from jax import lax
from jax.experimental import pallas as pl
from jax.experimental.pallas import tpu as pltpu
from jax.sharding import Mesh
from jax.sharding import PartitionSpec as P

F32, BF16 = jnp.float32, jnp.bfloat16
HEAD = 128
TOK = 128
PAIR = 2 * TOK
LINE = 8
SPAN = 4
OWN = 16
PART = OWN // SPAN
STATE = PART * HEAD
TAIL = 16
CTX = ("y", "x", "core")
VMEM_LIMIT = 16 << 20
HEAVY = 33
WEIGHTS = (32, 31)
CUTS = (0, 6, 8)


def mm(a, b, lhs, rhs):
    return lax.dot_general(a, b, (((lhs,), (rhs,)), ((), ())), preferred_element_type=F32)


def segment_of(bounds_ref, positions):
    total = jnp.zeros_like(positions)
    for j in range(bounds_ref.shape[0]):
        total = total + (bounds_ref[j] <= positions).astype(jnp.int32)
    return total


def scalar_segment(bounds_ref, position):
    total = jnp.int32(0)
    for j in range(bounds_ref.shape[0]):
        total = total + (bounds_ref[j] <= position).astype(jnp.int32)
    return total


def enter_columns(cum_t, bounds_ref, begin):
    positions = begin + lax.broadcasted_iota(jnp.int32, cum_t.shape, 0)
    same = segment_of(bounds_ref, positions) == scalar_segment(bounds_ref, begin - 1)
    return jnp.where(same, jnp.exp(cum_t), 0.0)


def leave_columns(cum_t, bounds_ref, begin):
    positions = begin + lax.broadcasted_iota(jnp.int32, cum_t.shape, 0)
    same = segment_of(bounds_ref, positions) == scalar_segment(bounds_ref, begin + PAIR - 1)
    return jnp.where(same, jnp.exp(cum_t[PAIR - 1 :, :] - cum_t), 0.0)


def head_cut(h):
    return slice(h * HEAD, (h + 1) * HEAD)


def pick_kernel(place_ref, gate_ref, *refs):
    core = place_ref[1]
    sources, (gate_keep, gate_send, keep_ref, send_ref) = refs[:4], refs[4:]
    for d in range(LINE):
        gate_keep[2 * d : 2 * d + 2, :] = gate_ref[2 * d + core]
        gate_send[2 * d : 2 * d + 2, :] = gate_ref[2 * d + 1 - core]
        for target, who in ((keep_ref, core), (send_ref, 1 - core)):
            lanes = pl.ds(pl.multiple_of((2 * d + who) * 2 * HEAD, 2 * HEAD), 2 * HEAD)
            for n, source in enumerate(sources):
                target[n, :, 2 * d * HEAD : 2 * (d + 1) * HEAD] = source[:, lanes]


def turn_kernel(x_ref, out_ref, hold):
    for j in range(x_ref.shape[1] // TOK):
        hold[j * TOK : (j + 1) * TOK, :] = x_ref[:, j * TOK : (j + 1) * TOK].T
    count, near = out_ref.shape[1:3]
    for j in range(count):
        for core in range(2):
            out_ref[core, j] = hold[(2 * j + core) * near : (2 * j + core + 1) * near, :]


def pair_kernel(place_ref, keep_ref, other_ref, out_ref):
    first = place_ref[1] == 0
    for half in range(2):
        keep, other = keep_ref[half], other_ref[half]
        out_ref[half, :, :TOK] = jnp.where(first, keep, other)
        out_ref[half, :, TOK:] = jnp.where(first, other, keep)


def other_kernel(place_ref, block_ref, out_ref):
    out_ref[...] = block_ref[1 - place_ref[1]]


def join(core, n, keep_ref, other_ref, out_ref):
    out_ref[pl.ds(pl.multiple_of(core * TOK, TOK), TOK), :] = keep_ref[n]
    out_ref[pl.ds(pl.multiple_of((1 - core) * TOK, TOK), TOK), :] = other_ref[n]


def states_kernel(place_ref, bounds_ref, *refs):
    gate_keep, gate_other, keep_ref, other_ref = refs[:4]
    out_refs, refs = refs[4 : 4 + SPAN], refs[4 + SPAN :]
    cum_ref, q_ref, g_ref, k_ref, v_ref, hold = refs
    begin, core = place_ref[0], place_ref[1]
    for n, ref in enumerate((q_ref, g_ref, k_ref, v_ref)):
        join(core, n, keep_ref, other_ref, ref)
    gates = (gate_keep[...], gate_other[...])
    swap = core == 1
    gate = jnp.concatenate(
        [jnp.where(swap, gates[1], gates[0]), jnp.where(swap, gates[0], gates[1])], axis=1
    )
    before = lax.broadcasted_iota(jnp.int32, (PAIR, PAIR), 0)
    after = lax.broadcasted_iota(jnp.int32, (PAIR, PAIR), 1)
    cum = jnp.dot(
        gate,
        (before <= after).astype(F32),
        precision=lax.Precision.HIGHEST,
        preferred_element_type=F32,
    )
    for d in range(LINE):
        cum_ref[d] = cum[2 * d : 2 * d + 2, :]
    enter = enter_columns(cum.T, bounds_ref, begin)
    leave = leave_columns(cum.T, bounds_ref, begin)
    rows = lax.broadcasted_iota(jnp.int32, (TAIL, HEAD), 0)
    for o in range(SPAN):
        tail = jnp.zeros((TAIL, HEAD), F32)
        for j in range(PART):
            h = o * PART + j
            weighted = (enter[:, h : h + 1] * q_ref[:, head_cut(h)].astype(F32)).astype(BF16)
            hold[o, head_cut(j), :] = mm(weighted, g_ref[:, head_cut(h)], 0, 0).astype(BF16)
            weighted = (leave[:, h : h + 1] * k_ref[:, head_cut(h)].astype(F32)).astype(BF16)
            hold[o, head_cut(PART + j), :] = mm(weighted, v_ref[:, head_cut(h)], 0, 0).astype(BF16)
            tail = jnp.where(rows == j, enter[PAIR - 1 :, h : h + 1], tail)
        hold[o, 2 * STATE :, :] = tail.astype(BF16)
    send_apart(place_ref[3], hold, out_refs)


def columns_of(cum_ref):
    return jnp.concatenate([cum_ref[d] for d in range(cum_ref.shape[0])], axis=0).T


def send_apart(place, hold, out_refs):
    for step, out_ref in enumerate(out_refs):
        out_ref[...] = hold[lax.rem(place + step, len(out_refs))]


def advance(state, hold, block, backward):
    pieces = []
    for j in range(PART):
        through = hold[block, 2 * STATE + j : 2 * STATE + j + 1, :].astype(F32)
        part = hold[block, head_cut(j if backward else PART + j), :].astype(F32)
        pieces.append(through * state[head_cut(j)] + part)
    return jnp.concatenate(pieces, axis=0)


def walk(backward):
    return reversed(range(SPAN)) if backward else range(SPAN)


def total_kernel(place_ref, *refs):
    parts, (back_ref, front_ref, sorted_ref) = refs[:SPAN], refs[SPAN:]
    take_in(place_ref[3], parts, sorted_ref)
    for backward, total_ref in ((True, back_ref), (False, front_ref)):
        state = jnp.zeros((STATE, HEAD), F32)
        for block in walk(backward):
            state = advance(state, sorted_ref, block, backward)
        total_ref[...] = state.astype(BF16)


def carry_kernel(place_ref, sorted_ref, back_ref, front_ref, *refs):
    out_refs, hold = refs[:SPAN], refs[SPAN]
    for backward, entry_ref in ((True, back_ref), (False, front_ref)):
        state = entry_ref[...].astype(F32)
        cut = slice(0, STATE) if backward else slice(STATE, 2 * STATE)
        for block in walk(backward):
            hold[block, cut, :] = state.astype(BF16)
            state = advance(state, sorted_ref, block, backward)
    send_apart(place_ref[3], hold, out_refs)


def take_in(lane, parts, hold):
    for step, part in enumerate(parts):
        hold[lax.rem(lane - step + SPAN, SPAN)] = part[...]


def inner_kernel(place_ref, bounds_ref, cum_ref, *refs):
    q_ref, k_ref, v_ref, g_ref, query_ref, key_ref, value_ref = refs
    begin = place_ref[0]
    cum = cum_ref[...]
    cum_t = cum.T
    row = lax.broadcasted_iota(jnp.int32, (PAIR, PAIR), 0)
    column = lax.broadcasted_iota(jnp.int32, (PAIR, PAIR), 1)
    row_ids = segment_of(bounds_ref, begin + lax.broadcasted_iota(jnp.int32, (PAIR, 1), 0))
    column_ids = segment_of(bounds_ref, begin + lax.broadcasted_iota(jnp.int32, (1, PAIR), 1))
    causal = (row >= column) & (row_ids == column_ids)
    for h in range(cum.shape[0]):
        cut = head_cut(h)
        decay = jnp.exp(jnp.where(causal, cum_t[:, h : h + 1] - cum[h : h + 1, :], -1e30))
        q, k, v, g = q_ref[:, cut], k_ref[:, cut], v_ref[:, cut], g_ref[:, cut]
        score_grad = (decay * mm(g, v, 1, 1)).astype(BF16)
        score_keys = (decay * mm(q, k, 1, 1)).astype(BF16)
        query_ref[:, cut] = mm(score_grad, k, 1, 0)
        key_ref[:, cut] = mm(score_grad, q, 0, 0)
        value_ref[:, cut] = mm(score_keys, g, 0, 0)


def piece_of(parts, h):
    for low, high, part in zip(CUTS, CUTS[1:], parts):
        if low <= h // 2 < high:
            return part[:, head_cut(h - 2 * low)]


def value_kernel(place_ref, bounds_ref, cum_ref, k_ref, *refs):
    value_in, states, refs = refs[:2], refs[2 : 2 + SPAN], refs[2 + SPAN :]
    send_ref, keep_ref, hold, out_hold = refs
    core, deep = place_ref[1], place_ref[2]
    take_in(place_ref[3], states, hold)
    leave = leave_columns(columns_of(cum_ref), bounds_ref, place_ref[0])
    for h in range(OWN):
        state = hold[h // PART, head_cut(h % PART), :]
        extra = leave[:, h : h + 1] * mm(k_ref[:, head_cut(h)], state, 1, 0)
        out_hold[h // 2, :, head_cut(h % 2)] = (piece_of(value_in, h) + extra).astype(BF16)
    for n, place in ((LINE // 2 - 1, deep), (LINE // 2, lax.rem(deep + LINE // 2, LINE))):
        keep_ref[n] = out_hold[place]
        send_ref[n] = out_hold[place]
    for n in range(LINE // 2 - 1):
        ahead, behind = lax.rem(deep + 1 + n, LINE), lax.rem(deep + LINE - 1 - n, LINE)
        keep_ref[n] = out_hold[jnp.where(core == 0, ahead, behind)]
        send_ref[n] = out_hold[jnp.where(core == 0, behind, ahead)]


def bundle_kernel(keep_ref, other_ref, *out_refs):
    for n, out_ref in enumerate(out_refs):
        out_ref[0] = keep_ref[n]
        out_ref[1] = other_ref[n]


def part_rows(core, value, cut, keep_ref, send_ref):
    keep_ref[:, cut] = jnp.where(core == 0, value[:TOK], value[TOK:]).astype(BF16)
    send_ref[:, cut] = jnp.where(core == 0, value[TOK:], value[:TOK]).astype(BF16)


def key_kernel(place_ref, bounds_ref, cum_ref, v_ref, *refs):
    key_in, states, (keep_ref, send_ref, hold) = refs[:2], refs[2 : 2 + SPAN], refs[2 + SPAN :]
    take_in(place_ref[3], states, hold)
    leave = leave_columns(columns_of(cum_ref), bounds_ref, place_ref[0])
    for h in range(OWN):
        state = hold[h // PART, head_cut(h % PART), :]
        extra = leave[:, h : h + 1] * mm(v_ref[:, head_cut(h)], state, 1, 1)
        part_rows(place_ref[1], piece_of(key_in, h) + extra, head_cut(h), keep_ref, send_ref)


def query_kernel(place_ref, bounds_ref, cum_ref, g_ref, *refs):
    query_in, states, (keep_ref, send_ref, hold) = refs[:2], refs[2 : 2 + SPAN], refs[2 + SPAN :]
    take_in(place_ref[3], states, hold)
    enter = enter_columns(columns_of(cum_ref), bounds_ref, place_ref[0])
    for h in range(OWN):
        state = hold[h // PART, head_cut(PART + h % PART), :]
        extra = enter[:, h : h + 1] * mm(g_ref[:, head_cut(h)], state, 1, 1)
        part_rows(place_ref[1], piece_of(query_in, h) + extra, head_cut(h), keep_ref, send_ref)


def lay_kernel(place_ref, keep_ref, other_ref, out_ref):
    core = place_ref[1]
    for d in range(LINE):
        near = slice(2 * d * HEAD, 2 * (d + 1) * HEAD)
        for source, who in ((keep_ref, core), (other_ref, 1 - core)):
            lanes = pl.ds(pl.multiple_of((2 * d + who) * 2 * HEAD, 2 * HEAD), 2 * HEAD)
            out_ref[:, lanes] = source[:, near]


def by_core(place_ref, keep, other):
    first = place_ref[1] == 0
    return jnp.concatenate([jnp.where(first, keep, other), jnp.where(first, other, keep)], axis=1)


def part_out(place_ref, rows, right, out_refs, hold):
    first, x, y = place_ref[1] == 0, place_ref[3], place_ref[4]
    near = hold.shape[1]
    tall = SPAN * near
    for j in range(SPAN):
        cut = slice(j * tall, (j + 1) * tall)
        acc = mm(rows[0][cut, :], right[0], 1, 0)
        for row, column in zip(rows[1:], right[1:], strict=True):
            acc = acc + mm(row[cut, :], column, 1, 0)
        acc = acc.astype(BF16)
        for i in range(SPAN):
            hold[j * SPAN + i] = acc[i * near : (i + 1) * near]
    for step, out_ref in enumerate(out_refs):
        there_x, there_y = lax.rem(x + step, SPAN), lax.rem(y + step, SPAN)
        for n in range(SPAN):
            out_ref[n] = hold[jnp.where(first, n * SPAN + there_x, there_y * SPAN + n)]


def far_kernel(place_ref, row_ref, pair_ref, *refs):
    right = by_core(place_ref, pair_ref[0], pair_ref[1])
    part_out(place_ref, [row_ref.at[place_ref[1]]], [right], refs[:SPAN], refs[SPAN])


def weight_kernel(place_ref, *refs):
    count = LINE // 2 - 1
    own_row, heres, theres, refs = refs[0], refs[1 : 1 + count], refs[1 + count : 1 + 2 * count], refs[1 + 2 * count :]
    own, near_refs, refs = refs[0], refs[1 : 1 + 2 * count], refs[1 + 2 * count :]
    core = place_ref[1]
    rows, right = [own_row.at[core]], [by_core(place_ref, own[0], own[1])]
    for n in range(count):
        here, there = near_refs[2 * n], near_refs[2 * n + 1]
        rows += [heres[n].at[core], theres[n]]
        right.append(by_core(place_ref, here[0], here[1]))
        right.append(by_core(place_ref, there[1], there[0]))
    part_out(place_ref, rows, right, refs[:SPAN], refs[SPAN])


def halfway_kernel(place_ref, *refs):
    parts, out_refs, hold = refs[:SPAN], refs[SPAN : 2 * SPAN], refs[2 * SPAN]
    for n in range(SPAN):
        total = parts[0][n].astype(F32)
        for part in parts[1:]:
            total = total + part[n].astype(F32)
        hold[n] = total.astype(BF16)
    send_apart(jnp.where(place_ref[1] == 0, place_ref[4], place_ref[3]), hold, out_refs)


def sum_kernel(*refs):
    parts, out_ref = refs[:-1], refs[-1]
    total = parts[0][...].astype(F32)
    for part in parts[1:]:
        total = total + part[...].astype(F32)
    out_ref[...] = total.astype(out_ref.dtype)


def shape(dims, dtype=BF16):
    return jax.ShapeDtypeStruct(dims, dtype)


def cost(heavy=0):
    return pl.CostEstimate(
        flops=1 << heavy, bytes_accessed=1, transcendentals=0
    )


def held(values, after):
    spec = pl.BlockSpec(memory_space=pl.ANY)
    return pl.pallas_call(
        lambda *refs: None,
        in_specs=[spec] * (len(values) + len(after)),
        out_specs=[spec] * len(values),
        out_shape=[shape(v.shape, v.dtype) for v in values],
        input_output_aliases={n: n for n in range(len(values))},
        compiler_params=pltpu.CompilerParams(vmem_limit_bytes=VMEM_LIMIT),
        cost_estimate=cost(),
    )(*values, *after)


def whole(kernel, smem, arrays, outs, scratch=(), after=(), heavy=0):
    vmem = pl.BlockSpec(memory_space=pltpu.VMEM)
    count = len(smem) + len(arrays)

    def body(*refs):
        kernel(*refs[:count], *refs[count + len(after) :])

    return pl.pallas_call(
        body,
        in_specs=[pl.BlockSpec(memory_space=pltpu.SMEM)] * len(smem)
        + [vmem] * len(arrays)
        + [pl.BlockSpec(memory_space=pl.ANY)] * len(after),
        out_specs=[vmem] * len(outs),
        out_shape=outs,
        scratch_shapes=list(scratch),
        compiler_params=pltpu.CompilerParams(vmem_limit_bytes=VMEM_LIMIT),
        cost_estimate=cost(heavy),
    )(*smem, *arrays, *after)


def inner(part, smem, cum, arrays, after):
    low, high = CUTS[part], CUTS[part + 1]
    outs = [shape((PAIR, (high - low) * 2 * HEAD), F32)] * 3
    count = len(smem) + 1 + len(arrays)

    def body(*refs):
        inner_kernel(*refs[:count], *refs[count + len(after) :])

    return pl.pallas_call(
        body,
        grid=(high - low,),
        in_specs=[pl.BlockSpec(memory_space=pltpu.SMEM)] * len(smem)
        + [pl.BlockSpec((None, 2, PAIR), lambda d: (d + low, 0, 0))]
        + [pl.BlockSpec((PAIR, 2 * HEAD), lambda d: (0, d + low))] * len(arrays)
        + [pl.BlockSpec(memory_space=pl.ANY)] * len(after),
        out_specs=[pl.BlockSpec((PAIR, 2 * HEAD), lambda d: (0, d))] * len(outs),
        out_shape=outs,
        compiler_params=pltpu.CompilerParams(vmem_limit_bytes=VMEM_LIMIT),
        cost_estimate=cost(WEIGHTS[part]),
    )(*smem, cum, *arrays, *after)


def shifted(value, axis, step):
    count = lax.axis_size(axis)
    return lax.ppermute(value, axis, [(i, (i + step) % count) for i in range(count)])


def swapped(value):
    return shifted(value, "core", 1)


def exchange(pieces, axis):
    return [pieces[0]] + [shifted(pieces[s], axis, s) for s in range(1, len(pieces))]


def apart(value, axes, moves):
    sizes = [lax.axis_size(a) for a in axes]
    pairs = []
    for place in itertools.product(*map(range, sizes)):
        for core, move in enumerate(moves):
            there = [(p + m) % n for p, m, n in zip(place, move, sizes, strict=True)]
            index = lambda at: functools.reduce(lambda t, pn: t * pn[1] + pn[0], zip(at, sizes), 0)
            pairs.append((2 * index(place) + core, 2 * index(there) + core))
    return lax.ppermute(value, (*axes, "core"), pairs)


def per_device(inputs, queries, keys, values, out_grad, log_gate, boundaries):
    q, k, v, g = queries[0], keys[0], values[0], out_grad[0]
    width = q.shape[1]
    model = inputs.shape[2]
    core, x, y = lax.axis_index("core"), lax.axis_index("x"), lax.axis_index("y")
    begin = (y * lax.axis_size("x") + x) * PAIR
    place = jnp.stack([begin, core, lax.axis_index("z"), x, y]).astype(jnp.int32)
    smem = (place, boundaries[0])
    plane = lax.axis_size("y") * lax.axis_size("x")
    count = lax.axis_size("y")
    half, chip = shape((TOK, width // 2)), shape((PAIR, width // 2))
    gate_half, cums = shape((OWN, TOK), F32), shape((LINE, 2, PAIR), F32)
    state, span = shape((STATE, HEAD)), (SPAN, 2 * STATE + TAIL, HEAD)
    hold_states = pltpu.VMEM((SPAN, 2 * STATE, HEAD), BF16)

    line = shape((2, plane, model // plane // 2, TOK))
    (turned,) = whole(turn_kernel, (), [inputs[0]], [line], [pltpu.VMEM((model, TOK), BF16)])
    turned_other = swapped(turned)
    (own,) = whole(
        pair_kernel,
        (place,),
        [a.reshape(2, model // 2, TOK) for a in (turned, turned_other)],
        [shape((2, model // 2, PAIR))],
    )
    step = lambda block: apart(block, ("z",), [(1,), (-1,)])
    ring_1 = step(own)
    gate_keep, gate_send, keep, send = whole(
        pick_kernel,
        (place,),
        [log_gate[0].reshape(OWN, 2, TOK), q, g, k, v],
        [gate_half] * 2 + [shape((4, *half.shape))] * 2,
        after=[own],
        heavy=HEAVY,
    )
    *parts, cum, q, g, k, v = whole(
        states_kernel,
        smem,
        [gate_keep, swapped(gate_send), keep, swapped(send)],
        [shape(span[1:])] * SPAN + [cums] + [chip] * 4,
        [pltpu.VMEM(span, BF16)],
    )
    parts = exchange(parts, "x")
    inner_1 = inner(0, smem, cum, [q, k, v, g], [])
    parts = held(parts, [inner_1[0]])
    (ring_1,) = held([ring_1], [parts[1]])
    ring_2 = step(ring_1)
    back, front, parts = whole(total_kernel, (place,), parts, [state, state, shape(span)])
    back = lax.ppermute(back, "y", [(i + 1, i) for i in range(count - 1)])
    front = lax.ppermute(front, "y", [(i, i + 1) for i in range(count - 1)])
    carried = whole(
        carry_kernel,
        (place,),
        [parts, back, front],
        [shape((2 * STATE, HEAD))] * SPAN,
        [hold_states],
    )
    inner_2 = inner(1, smem, cum, [q, k, v, g], [carried[0]])
    carried = exchange(carried, "x")
    (ring_2,) = held([ring_2], [inner_2[0]])
    ring_3 = step(ring_2)
    carried = held(carried, [ring_2])
    query_in, key_in, value_in = zip(inner_1, inner_2)
    several = shape((LINE // 2 + 1, PAIR, 2 * HEAD))
    send, keep = whole(
        value_kernel,
        smem,
        [cum, k, *value_in, *carried],
        [several, several],
        [hold_states, pltpu.VMEM((LINE, PAIR, 2 * HEAD), BF16)],
        heavy=HEAVY,
    )
    *bundles, own_part, far_part = whole(
        bundle_kernel, (), [keep, swapped(send)], [shape((2, PAIR, 2 * HEAD))] * (LINE // 2 + 1)
    )
    started = bundles[0]
    bundles = [apart(b, ("z",), [(n + 1,), (-n - 1,)]) for n, b in enumerate(bundles)]
    key_keep, key_send = whole(
        key_kernel,
        smem,
        [cum, v, *key_in, *carried],
        [half] * 2,
        [hold_states],
        after=[started],
        heavy=29,
    )
    key_other = swapped(key_send)
    near = model // plane // 2
    pieces = [shape((SPAN, near, 4 * HEAD))] * SPAN
    hold_rows = pltpu.VMEM((plane, near, 4 * HEAD), BF16)
    far = whole(far_kernel, (place,), [own, far_part], pieces, [hold_rows], after=[key_send, ring_3])

    def one_way(parts):
        moved = [apart(parts[n], ("y", "x"), [(0, n), (n, 0)]) for n in range(1, SPAN)]
        return [parts[0], *moved]

    def other_way(parts):
        moved = [apart(parts[n], ("y", "x"), [(n, 0), (0, n)]) for n in range(1, SPAN)]
        return [parts[0], *moved]

    def halfway(parts):
        return whole(
            halfway_kernel,
            (place,),
            parts,
            [shape((near, 4 * HEAD))] * SPAN,
            [pltpu.VMEM((SPAN, near, 4 * HEAD), BF16)],
        )

    far = halfway(one_way(far))
    rings = [ring_1, ring_2, ring_3]
    others = [
        swapped(whole(other_kernel, (place,), [r], [shape((model // 2, PAIR))])[0]) for r in rings
    ]
    columns = [own_part]
    for b in bundles:
        columns += [b, swapped(b)]
    parts = whole(
        weight_kernel,
        (place,),
        [own, *rings, *others, *columns],
        pieces,
        [hold_rows],
        after=[key_send, far[0]],
    )
    started = parts[0]
    parts = one_way(parts)
    query_keep, query_send = whole(
        query_kernel,
        smem,
        [cum, g, *query_in, *carried],
        [half] * 2,
        [hold_states],
        after=[started],
        heavy=HEAVY,
    )
    query_other = swapped(query_send)
    far = other_way(held(far, [query_send]))
    (far,) = whole(sum_kernel, (), far, [shape((near, 4 * HEAD))])
    far = apart(far, ("z",), [(LINE // 2,), (LINE // 2,)])
    (key_grad,) = whole(
        lay_kernel, (place,), [key_keep, key_other], [shape((TOK, width))], after=[started], heavy=HEAVY
    )
    parts = halfway(held(parts, [key_grad]))
    started = parts[0]
    parts = other_way(parts)
    (query_grad,) = whole(
        lay_kernel,
        (place,),
        [query_keep, query_other],
        [shape((TOK, width))],
        after=[started],
        heavy=HEAVY,
    )
    parts = held(parts, [query_grad])
    (weight,) = whole(sum_kernel, (), [*parts, far], [shape((near, 4 * HEAD), F32)])
    return query_grad[None], key_grad[None], weight


def solution(mesh):
    fine = Mesh(mesh.devices.reshape(LINE, 4, SPAN, 2), ("z", "y", "x", "core"))
    rows = P("z", CTX, None)
    in_specs = (rows, rows, rows, rows, rows, P("z", None, CTX), P("z", None))
    out_specs = (rows, rows, P(CTX, "z"))
    return jax.shard_map(
        per_device, mesh=fine, in_specs=in_specs, out_specs=out_specs, check_vma=False
    )
```

```python
import functools
import itertools

import jax
import jax.numpy as jnp
from jax import lax
from jax.experimental import pallas as pl
from jax.experimental.pallas import tpu as pltpu
from jax.sharding import Mesh
from jax.sharding import PartitionSpec as P

F32, BF16 = jnp.float32, jnp.bfloat16
HEAD = 128
TOK = 128
PAIR = 2 * TOK
LINE = 8
SPAN = 4
OWN = 16
PART = OWN // SPAN
STATE = PART * HEAD
TAIL = 16
CTX = ("y", "x", "core")
VMEM_LIMIT = 16 << 20
HEAVY = 33
WEIGHTS = (32, 31)
CUTS = (0, 6, 8)


def mm(a, b, lhs, rhs):
    return lax.dot_general(a, b, (((lhs,), (rhs,)), ((), ())), preferred_element_type=F32)


def segment_of(bounds_ref, positions):
    total = jnp.zeros_like(positions)
    for j in range(bounds_ref.shape[0]):
        total = total + (bounds_ref[j] <= positions).astype(jnp.int32)
    return total


def scalar_segment(bounds_ref, position):
    total = jnp.int32(0)
    for j in range(bounds_ref.shape[0]):
        total = total + (bounds_ref[j] <= position).astype(jnp.int32)
    return total


def enter_columns(cum_t, bounds_ref, begin):
    positions = begin + lax.broadcasted_iota(jnp.int32, cum_t.shape, 0)
    same = segment_of(bounds_ref, positions) == scalar_segment(bounds_ref, begin - 1)
    return jnp.where(same, jnp.exp(cum_t), 0.0)


def leave_columns(cum_t, bounds_ref, begin):
    positions = begin + lax.broadcasted_iota(jnp.int32, cum_t.shape, 0)
    same = segment_of(bounds_ref, positions) == scalar_segment(bounds_ref, begin + PAIR - 1)
    return jnp.where(same, jnp.exp(cum_t[PAIR - 1 :, :] - cum_t), 0.0)


def head_cut(h):
    return slice(h * HEAD, (h + 1) * HEAD)


def pick_kernel(place_ref, gate_ref, *refs):
    core = place_ref[1]
    sources, (gate_keep, gate_send, keep_ref, send_ref) = refs[:4], refs[4:]
    for d in range(LINE):
        gate_keep[2 * d : 2 * d + 2, :] = gate_ref[2 * d + core]
        gate_send[2 * d : 2 * d + 2, :] = gate_ref[2 * d + 1 - core]
        for target, who in ((keep_ref, core), (send_ref, 1 - core)):
            lanes = pl.ds(pl.multiple_of((2 * d + who) * 2 * HEAD, 2 * HEAD), 2 * HEAD)
            for n, source in enumerate(sources):
                target[n, :, 2 * d * HEAD : 2 * (d + 1) * HEAD] = source[:, lanes]


def turn_kernel(x_ref, out_ref, hold):
    for j in range(x_ref.shape[1] // TOK):
        hold[j * TOK : (j + 1) * TOK, :] = x_ref[:, j * TOK : (j + 1) * TOK].T
    count, near = out_ref.shape[1:3]
    for j in range(count):
        for core in range(2):
            out_ref[core, j] = hold[(2 * j + core) * near : (2 * j + core + 1) * near, :]


def pair_kernel(place_ref, keep_ref, other_ref, out_ref):
    first = place_ref[1] == 0
    for half in range(2):
        keep, other = keep_ref[half], other_ref[half]
        out_ref[half, :, :TOK] = jnp.where(first, keep, other)
        out_ref[half, :, TOK:] = jnp.where(first, other, keep)


def other_kernel(place_ref, block_ref, out_ref):
    out_ref[...] = block_ref[1 - place_ref[1]]


def join(core, n, keep_ref, other_ref, out_ref):
    out_ref[pl.ds(pl.multiple_of(core * TOK, TOK), TOK), :] = keep_ref[n]
    out_ref[pl.ds(pl.multiple_of((1 - core) * TOK, TOK), TOK), :] = other_ref[n]


def states_kernel(place_ref, bounds_ref, *refs):
    gate_keep, gate_other, keep_ref, other_ref = refs[:4]
    out_refs, refs = refs[4 : 4 + SPAN], refs[4 + SPAN :]
    cum_ref, q_ref, g_ref, k_ref, v_ref, hold = refs
    begin, core = place_ref[0], place_ref[1]
    for n, ref in enumerate((q_ref, g_ref, k_ref, v_ref)):
        join(core, n, keep_ref, other_ref, ref)
    gates = (gate_keep[...], gate_other[...])
    swap = core == 1
    gate = jnp.concatenate(
        [jnp.where(swap, gates[1], gates[0]), jnp.where(swap, gates[0], gates[1])], axis=1
    )
    before = lax.broadcasted_iota(jnp.int32, (PAIR, PAIR), 0)
    after = lax.broadcasted_iota(jnp.int32, (PAIR, PAIR), 1)
    cum = jnp.dot(
        gate,
        (before <= after).astype(F32),
        precision=lax.Precision.HIGHEST,
        preferred_element_type=F32,
    )
    for d in range(LINE):
        cum_ref[d] = cum[2 * d : 2 * d + 2, :]
    enter = enter_columns(cum.T, bounds_ref, begin)
    leave = leave_columns(cum.T, bounds_ref, begin)
    rows = lax.broadcasted_iota(jnp.int32, (TAIL, HEAD), 0)
    for o in range(SPAN):
        tail = jnp.zeros((TAIL, HEAD), F32)
        for j in range(PART):
            h = o * PART + j
            weighted = (enter[:, h : h + 1] * q_ref[:, head_cut(h)].astype(F32)).astype(BF16)
            hold[o, head_cut(j), :] = mm(weighted, g_ref[:, head_cut(h)], 0, 0).astype(BF16)
            weighted = (leave[:, h : h + 1] * k_ref[:, head_cut(h)].astype(F32)).astype(BF16)
            hold[o, head_cut(PART + j), :] = mm(weighted, v_ref[:, head_cut(h)], 0, 0).astype(BF16)
            tail = jnp.where(rows == j, enter[PAIR - 1 :, h : h + 1], tail)
        hold[o, 2 * STATE :, :] = tail.astype(BF16)
    send_apart(place_ref[3], hold, out_refs)


def columns_of(cum_ref):
    return jnp.concatenate([cum_ref[d] for d in range(cum_ref.shape[0])], axis=0).T


def send_apart(place, hold, out_refs):
    for step, out_ref in enumerate(out_refs):
        out_ref[...] = hold[lax.rem(place + step, len(out_refs))]


def advance(state, hold, block, backward):
    pieces = []
    for j in range(PART):
        through = hold[block, 2 * STATE + j : 2 * STATE + j + 1, :].astype(F32)
        part = hold[block, head_cut(j if backward else PART + j), :].astype(F32)
        pieces.append(through * state[head_cut(j)] + part)
    return jnp.concatenate(pieces, axis=0)


def walk(backward):
    return reversed(range(SPAN)) if backward else range(SPAN)


def total_kernel(place_ref, *refs):
    parts, (back_ref, front_ref, sorted_ref) = refs[:SPAN], refs[SPAN:]
    take_in(place_ref[3], parts, sorted_ref)
    for backward, total_ref in ((True, back_ref), (False, front_ref)):
        state = jnp.zeros((STATE, HEAD), F32)
        for block in walk(backward):
            state = advance(state, sorted_ref, block, backward)
        total_ref[...] = state.astype(BF16)


def carry_kernel(place_ref, sorted_ref, back_ref, front_ref, *refs):
    out_refs, hold = refs[:SPAN], refs[SPAN]
    for backward, entry_ref in ((True, back_ref), (False, front_ref)):
        state = entry_ref[...].astype(F32)
        cut = slice(0, STATE) if backward else slice(STATE, 2 * STATE)
        for block in walk(backward):
            hold[block, cut, :] = state.astype(BF16)
            state = advance(state, sorted_ref, block, backward)
    send_apart(place_ref[3], hold, out_refs)


def take_in(lane, parts, hold):
    for step, part in enumerate(parts):
        hold[lax.rem(lane - step + SPAN, SPAN)] = part[...]


def inner_kernel(place_ref, bounds_ref, cum_ref, *refs):
    q_ref, k_ref, v_ref, g_ref, query_ref, key_ref, value_ref = refs
    begin = place_ref[0]
    cum = cum_ref[...]
    cum_t = cum.T
    row = lax.broadcasted_iota(jnp.int32, (PAIR, PAIR), 0)
    column = lax.broadcasted_iota(jnp.int32, (PAIR, PAIR), 1)
    row_ids = segment_of(bounds_ref, begin + lax.broadcasted_iota(jnp.int32, (PAIR, 1), 0))
    column_ids = segment_of(bounds_ref, begin + lax.broadcasted_iota(jnp.int32, (1, PAIR), 1))
    causal = (row >= column) & (row_ids == column_ids)
    for h in range(cum.shape[0]):
        cut = head_cut(h)
        decay = jnp.exp(jnp.where(causal, cum_t[:, h : h + 1] - cum[h : h + 1, :], -1e30))
        q, k, v, g = q_ref[:, cut], k_ref[:, cut], v_ref[:, cut], g_ref[:, cut]
        score_grad = (decay * mm(g, v, 1, 1)).astype(BF16)
        score_keys = (decay * mm(q, k, 1, 1)).astype(BF16)
        query_ref[:, cut] = mm(score_grad, k, 1, 0)
        key_ref[:, cut] = mm(score_grad, q, 0, 0)
        value_ref[:, cut] = mm(score_keys, g, 0, 0)


def piece_of(parts, h):
    for low, high, part in zip(CUTS, CUTS[1:], parts):
        if low <= h // 2 < high:
            return part[:, head_cut(h - 2 * low)]


def value_kernel(place_ref, bounds_ref, cum_ref, k_ref, *refs):
    value_in, states, refs = refs[:2], refs[2 : 2 + SPAN], refs[2 + SPAN :]
    send_ref, keep_ref, hold, out_hold = refs
    core, deep = place_ref[1], place_ref[2]
    take_in(place_ref[3], states, hold)
    leave = leave_columns(columns_of(cum_ref), bounds_ref, place_ref[0])
    for h in range(OWN):
        state = hold[h // PART, head_cut(h % PART), :]
        extra = leave[:, h : h + 1] * mm(k_ref[:, head_cut(h)], state, 1, 0)
        out_hold[h // 2, :, head_cut(h % 2)] = (piece_of(value_in, h) + extra).astype(BF16)
    keep_ref[LINE // 2 - 1] = out_hold[deep]
    send_ref[LINE // 2 - 1] = out_hold[deep]
    keep_ref[LINE // 2] = out_hold[lax.rem(deep + LINE // 2, LINE)]
    for n in range(LINE // 2 - 1):
        ahead, behind = lax.rem(deep + 1 + n, LINE), lax.rem(deep + LINE - 1 - n, LINE)
        keep_ref[n] = out_hold[jnp.where(core == 0, ahead, behind)]
        send_ref[n] = out_hold[jnp.where(core == 0, behind, ahead)]


def bundle_kernel(keep_ref, other_ref, *out_refs):
    for n, out_ref in enumerate(out_refs[:-1]):
        out_ref[0] = keep_ref[n]
        out_ref[1] = other_ref[n]
    out_refs[-1][...] = keep_ref[len(out_refs) - 1]


def part_rows(core, value, cut, keep_ref, send_ref):
    keep_ref[:, cut] = jnp.where(core == 0, value[:TOK], value[TOK:]).astype(BF16)
    send_ref[:, cut] = jnp.where(core == 0, value[TOK:], value[:TOK]).astype(BF16)


def key_kernel(place_ref, bounds_ref, cum_ref, v_ref, *refs):
    key_in, states, (keep_ref, send_ref, hold) = refs[:2], refs[2 : 2 + SPAN], refs[2 + SPAN :]
    take_in(place_ref[3], states, hold)
    leave = leave_columns(columns_of(cum_ref), bounds_ref, place_ref[0])
    for h in range(OWN):
        state = hold[h // PART, head_cut(h % PART), :]
        extra = leave[:, h : h + 1] * mm(v_ref[:, head_cut(h)], state, 1, 1)
        part_rows(place_ref[1], piece_of(key_in, h) + extra, head_cut(h), keep_ref, send_ref)


def query_kernel(place_ref, bounds_ref, cum_ref, g_ref, *refs):
    query_in, states, (keep_ref, send_ref, hold) = refs[:2], refs[2 : 2 + SPAN], refs[2 + SPAN :]
    take_in(place_ref[3], states, hold)
    enter = enter_columns(columns_of(cum_ref), bounds_ref, place_ref[0])
    for h in range(OWN):
        state = hold[h // PART, head_cut(PART + h % PART), :]
        extra = enter[:, h : h + 1] * mm(g_ref[:, head_cut(h)], state, 1, 1)
        part_rows(place_ref[1], piece_of(query_in, h) + extra, head_cut(h), keep_ref, send_ref)


def lay_kernel(place_ref, keep_ref, other_ref, out_ref):
    core = place_ref[1]
    for d in range(LINE):
        near = slice(2 * d * HEAD, 2 * (d + 1) * HEAD)
        for source, who in ((keep_ref, core), (other_ref, 1 - core)):
            lanes = pl.ds(pl.multiple_of((2 * d + who) * 2 * HEAD, 2 * HEAD), 2 * HEAD)
            out_ref[:, lanes] = source[:, near]


def by_core(place_ref, keep, other):
    first = place_ref[1] == 0
    return jnp.concatenate([jnp.where(first, keep, other), jnp.where(first, other, keep)], axis=1)


def part_out(place_ref, rows, right, out_refs, hold):
    first, x, y = place_ref[1] == 0, place_ref[3], place_ref[4]
    near = hold.shape[1]
    tall = SPAN * near
    for j in range(SPAN):
        cut = slice(j * tall, (j + 1) * tall)
        acc = mm(rows[0][cut, :], right[0], 1, 0)
        for row, column in zip(rows[1:], right[1:], strict=True):
            acc = acc + mm(row[cut, :], column, 1, 0)
        acc = acc.astype(BF16)
        for i in range(SPAN):
            hold[j * SPAN + i] = acc[i * near : (i + 1) * near]
    for step, out_ref in enumerate(out_refs):
        there_x, there_y = lax.rem(x + step, SPAN), lax.rem(y + step, SPAN)
        for n in range(SPAN):
            out_ref[n] = hold[jnp.where(first, n * SPAN + there_x, there_y * SPAN + n)]


def mine_kernel(place_ref, block_ref, out_ref):
    out_ref[...] = block_ref[place_ref[1]]


def weight_kernel(place_ref, *refs):
    count = LINE // 2 - 1
    own_row, heres, theres, refs = refs[0], refs[1 : 1 + count], refs[1 + count : 1 + 2 * count], refs[1 + 2 * count :]
    far_row, far, far_other = refs[:3]
    own, near_refs, refs = refs[3], refs[4 : 4 + 2 * count], refs[4 + 2 * count :]
    core = place_ref[1]
    rows, right = [own_row.at[core]], [by_core(place_ref, own[0], own[1])]
    for n in range(count):
        here, there = near_refs[2 * n], near_refs[2 * n + 1]
        rows += [heres[n].at[core], theres[n]]
        right.append(by_core(place_ref, here[0], here[1]))
        right.append(by_core(place_ref, there[1], there[0]))
    rows.append(far_row)
    right.append(by_core(place_ref, far[...], far_other[...]))
    part_out(place_ref, rows, right, refs[:SPAN], refs[SPAN])


def halfway_kernel(place_ref, *refs):
    parts, out_refs, hold = refs[:SPAN], refs[SPAN : 2 * SPAN], refs[2 * SPAN]
    for n in range(SPAN):
        total = parts[0][n].astype(F32)
        for part in parts[1:]:
            total = total + part[n].astype(F32)
        hold[n] = total.astype(BF16)
    send_apart(jnp.where(place_ref[1] == 0, place_ref[4], place_ref[3]), hold, out_refs)


def sum_kernel(*refs):
    parts, out_ref = refs[:-1], refs[-1]
    total = parts[0][...].astype(F32)
    for part in parts[1:]:
        total = total + part[...].astype(F32)
    out_ref[...] = total.astype(out_ref.dtype)


def shape(dims, dtype=BF16):
    return jax.ShapeDtypeStruct(dims, dtype)


def cost(heavy=0):
    return pl.CostEstimate(
        flops=1 << heavy, bytes_accessed=1, transcendentals=0
    )


def held(values, after):
    spec = pl.BlockSpec(memory_space=pl.ANY)
    return pl.pallas_call(
        lambda *refs: None,
        in_specs=[spec] * (len(values) + len(after)),
        out_specs=[spec] * len(values),
        out_shape=[shape(v.shape, v.dtype) for v in values],
        input_output_aliases={n: n for n in range(len(values))},
        compiler_params=pltpu.CompilerParams(vmem_limit_bytes=VMEM_LIMIT),
        cost_estimate=cost(),
    )(*values, *after)


def whole(kernel, smem, arrays, outs, scratch=(), after=(), heavy=0):
    vmem = pl.BlockSpec(memory_space=pltpu.VMEM)
    count = len(smem) + len(arrays)

    def body(*refs):
        kernel(*refs[:count], *refs[count + len(after) :])

    return pl.pallas_call(
        body,
        in_specs=[pl.BlockSpec(memory_space=pltpu.SMEM)] * len(smem)
        + [vmem] * len(arrays)
        + [pl.BlockSpec(memory_space=pl.ANY)] * len(after),
        out_specs=[vmem] * len(outs),
        out_shape=outs,
        scratch_shapes=list(scratch),
        compiler_params=pltpu.CompilerParams(vmem_limit_bytes=VMEM_LIMIT),
        cost_estimate=cost(heavy),
    )(*smem, *arrays, *after)


def inner(part, smem, cum, arrays, after):
    low, high = CUTS[part], CUTS[part + 1]
    outs = [shape((PAIR, (high - low) * 2 * HEAD), F32)] * 3
    count = len(smem) + 1 + len(arrays)

    def body(*refs):
        inner_kernel(*refs[:count], *refs[count + len(after) :])

    return pl.pallas_call(
        body,
        grid=(high - low,),
        in_specs=[pl.BlockSpec(memory_space=pltpu.SMEM)] * len(smem)
        + [pl.BlockSpec((None, 2, PAIR), lambda d: (d + low, 0, 0))]
        + [pl.BlockSpec((PAIR, 2 * HEAD), lambda d: (0, d + low))] * len(arrays)
        + [pl.BlockSpec(memory_space=pl.ANY)] * len(after),
        out_specs=[pl.BlockSpec((PAIR, 2 * HEAD), lambda d: (0, d))] * len(outs),
        out_shape=outs,
        compiler_params=pltpu.CompilerParams(vmem_limit_bytes=VMEM_LIMIT),
        cost_estimate=cost(WEIGHTS[part]),
    )(*smem, cum, *arrays, *after)


def shifted(value, axis, step):
    count = lax.axis_size(axis)
    return lax.ppermute(value, axis, [(i, (i + step) % count) for i in range(count)])


def swapped(value):
    return shifted(value, "core", 1)


def exchange(pieces, axis):
    return [pieces[0]] + [shifted(pieces[s], axis, s) for s in range(1, len(pieces))]


def apart(value, axes, moves):
    sizes = [lax.axis_size(a) for a in axes]
    pairs = []
    for place in itertools.product(*map(range, sizes)):
        for core, move in enumerate(moves):
            there = [(p + m) % n for p, m, n in zip(place, move, sizes, strict=True)]
            index = lambda at: functools.reduce(lambda t, pn: t * pn[1] + pn[0], zip(at, sizes), 0)
            pairs.append((2 * index(place) + core, 2 * index(there) + core))
    return lax.ppermute(value, (*axes, "core"), pairs)


def per_device(inputs, queries, keys, values, out_grad, log_gate, boundaries):
    q, k, v, g = queries[0], keys[0], values[0], out_grad[0]
    width = q.shape[1]
    model = inputs.shape[2]
    core, x, y = lax.axis_index("core"), lax.axis_index("x"), lax.axis_index("y")
    begin = (y * lax.axis_size("x") + x) * PAIR
    place = jnp.stack([begin, core, lax.axis_index("z"), x, y]).astype(jnp.int32)
    smem = (place, boundaries[0])
    plane = lax.axis_size("y") * lax.axis_size("x")
    count = lax.axis_size("y")
    half, chip = shape((TOK, width // 2)), shape((PAIR, width // 2))
    gate_half, cums = shape((OWN, TOK), F32), shape((LINE, 2, PAIR), F32)
    state, span = shape((STATE, HEAD)), (SPAN, 2 * STATE + TAIL, HEAD)
    hold_states = pltpu.VMEM((SPAN, 2 * STATE, HEAD), BF16)

    line = shape((2, plane, model // plane // 2, TOK))
    (turned,) = whole(turn_kernel, (), [inputs[0]], [line], [pltpu.VMEM((model, TOK), BF16)])
    turned_other = swapped(turned)
    (own,) = whole(
        pair_kernel,
        (place,),
        [a.reshape(2, model // 2, TOK) for a in (turned, turned_other)],
        [shape((2, model // 2, PAIR))],
    )
    step = lambda block: apart(block, ("z",), [(1,), (-1,)])
    ring_1 = step(own)
    gate_keep, gate_send, keep, send = whole(
        pick_kernel,
        (place,),
        [log_gate[0].reshape(OWN, 2, TOK), q, g, k, v],
        [gate_half] * 2 + [shape((4, *half.shape))] * 2,
        after=[own],
        heavy=HEAVY,
    )
    *parts, cum, q, g, k, v = whole(
        states_kernel,
        smem,
        [gate_keep, swapped(gate_send), keep, swapped(send)],
        [shape(span[1:])] * SPAN + [cums] + [chip] * 4,
        [pltpu.VMEM(span, BF16)],
    )
    parts = exchange(parts, "x")
    inner_1 = inner(0, smem, cum, [q, k, v, g], [])
    parts = held(parts, [inner_1[0]])
    (ring_1,) = held([ring_1], [parts[1]])
    ring_2 = step(ring_1)
    back, front, parts = whole(total_kernel, (place,), parts, [state, state, shape(span)])
    back = lax.ppermute(back, "y", [(i + 1, i) for i in range(count - 1)])
    front = lax.ppermute(front, "y", [(i, i + 1) for i in range(count - 1)])
    carried = whole(
        carry_kernel,
        (place,),
        [parts, back, front],
        [shape((2 * STATE, HEAD))] * SPAN,
        [hold_states],
    )
    inner_2 = inner(1, smem, cum, [q, k, v, g], [carried[0]])
    carried = exchange(carried, "x")
    (ring_2,) = held([ring_2], [inner_2[0]])
    ring_3 = step(ring_2)
    carried = held(carried, [ring_2])
    query_in, key_in, value_in = zip(inner_1, inner_2)
    several = [shape((n, PAIR, 2 * HEAD)) for n in (LINE // 2, LINE // 2 + 1)]
    send, keep = whole(
        value_kernel,
        smem,
        [cum, k, *value_in, *carried],
        several,
        [hold_states, pltpu.VMEM((LINE, PAIR, 2 * HEAD), BF16)],
        heavy=HEAVY,
    )
    *bundles, own_part, far_part = whole(
        bundle_kernel,
        (),
        [keep, swapped(send)],
        [shape((2, PAIR, 2 * HEAD))] * (LINE // 2) + [shape((PAIR, 2 * HEAD))],
    )
    started = bundles[0]
    bundles = [apart(b, ("z",), [(n + 1,), (-n - 1,)]) for n, b in enumerate(bundles)]
    far_part = apart(far_part, ("z",), [(LINE // 2,), (LINE // 2,)])
    key_keep, key_send = whole(
        key_kernel,
        smem,
        [cum, v, *key_in, *carried],
        [half] * 2,
        [hold_states],
        after=[started],
        heavy=29,
    )
    key_other = swapped(key_send)
    near = model // plane // 2
    pieces = [shape((SPAN, near, 4 * HEAD))] * SPAN
    hold_rows = pltpu.VMEM((plane, near, 4 * HEAD), BF16)
    (mine,) = whole(
        mine_kernel, (place,), [ring_3], [shape((model // 2, PAIR))], after=[key_send]
    )
    ring_4 = step(mine)

    def one_way(parts):
        moved = [apart(parts[n], ("y", "x"), [(0, n), (n, 0)]) for n in range(1, SPAN)]
        return [parts[0], *moved]

    def other_way(parts):
        moved = [apart(parts[n], ("y", "x"), [(n, 0), (0, n)]) for n in range(1, SPAN)]
        return [parts[0], *moved]

    def halfway(parts):
        return whole(
            halfway_kernel,
            (place,),
            parts,
            [shape((near, 4 * HEAD))] * SPAN,
            [pltpu.VMEM((SPAN, near, 4 * HEAD), BF16)],
        )

    rings = [ring_1, ring_2, ring_3]
    others = [
        swapped(whole(other_kernel, (place,), [r], [shape((model // 2, PAIR))])[0]) for r in rings
    ]
    columns = [own_part]
    for b in bundles:
        columns += [b, swapped(b)]
    parts = whole(
        weight_kernel,
        (place,),
        [own, *rings, *others, ring_4, far_part, swapped(far_part), *columns],
        pieces,
        [hold_rows],
        after=[key_send],
    )
    started = parts[0]
    parts = one_way(parts)
    query_keep, query_send = whole(
        query_kernel,
        smem,
        [cum, g, *query_in, *carried],
        [half] * 2,
        [hold_states],
        after=[started],
        heavy=HEAVY,
    )
    query_other = swapped(query_send)
    (key_grad,) = whole(
        lay_kernel, (place,), [key_keep, key_other], [shape((TOK, width))], after=[started], heavy=HEAVY
    )
    parts = halfway(held(parts, [key_grad]))
    started = parts[0]
    parts = other_way(parts)
    (query_grad,) = whole(
        lay_kernel,
        (place,),
        [query_keep, query_other],
        [shape((TOK, width))],
        after=[started],
        heavy=HEAVY,
    )
    parts = held(parts, [query_grad])
    (weight,) = whole(sum_kernel, (), parts, [shape((near, 4 * HEAD), F32)])
    return query_grad[None], key_grad[None], weight


def solution(mesh):
    fine = Mesh(mesh.devices.reshape(LINE, 4, SPAN, 2), ("z", "y", "x", "core"))
    rows = P("z", CTX, None)
    in_specs = (rows, rows, rows, rows, rows, P("z", None, CTX), P("z", None))
    out_specs = (rows, rows, P(CTX, "z"))
    return jax.shard_map(
        per_device, mesh=fine, in_specs=in_specs, out_specs=out_specs, check_vma=False
    )
```

```python
import functools
import itertools

import jax
import jax.numpy as jnp
from jax import lax
from jax.experimental import pallas as pl
from jax.experimental.pallas import tpu as pltpu
from jax.sharding import Mesh
from jax.sharding import PartitionSpec as P

F32, BF16 = jnp.float32, jnp.bfloat16
HEAD = 128
TOK = 128
PAIR = 2 * TOK
LINE = 8
SPAN = 4
OWN = 16
PART = OWN // SPAN
STATE = PART * HEAD
TAIL = 16
CTX = ("y", "x", "core")
VMEM_LIMIT = 16 << 20
HEAVY = 33
WEIGHTS = (32, 31)
CUTS = (0, 6, 8)


def mm(a, b, lhs, rhs):
    return lax.dot_general(a, b, (((lhs,), (rhs,)), ((), ())), preferred_element_type=F32)


def segment_of(bounds_ref, positions):
    total = jnp.zeros_like(positions)
    for j in range(bounds_ref.shape[0]):
        total = total + (bounds_ref[j] <= positions).astype(jnp.int32)
    return total


def scalar_segment(bounds_ref, position):
    total = jnp.int32(0)
    for j in range(bounds_ref.shape[0]):
        total = total + (bounds_ref[j] <= position).astype(jnp.int32)
    return total


def enter_columns(cum_t, bounds_ref, begin):
    positions = begin + lax.broadcasted_iota(jnp.int32, cum_t.shape, 0)
    same = segment_of(bounds_ref, positions) == scalar_segment(bounds_ref, begin - 1)
    return jnp.where(same, jnp.exp(cum_t), 0.0)


def leave_columns(cum_t, bounds_ref, begin):
    positions = begin + lax.broadcasted_iota(jnp.int32, cum_t.shape, 0)
    same = segment_of(bounds_ref, positions) == scalar_segment(bounds_ref, begin + PAIR - 1)
    return jnp.where(same, jnp.exp(cum_t[PAIR - 1 :, :] - cum_t), 0.0)


def head_cut(h):
    return slice(h * HEAD, (h + 1) * HEAD)


def pick_kernel(place_ref, gate_ref, *refs):
    core = place_ref[1]
    sources, (gate_keep, gate_send, keep_ref, send_ref) = refs[:4], refs[4:]
    for d in range(LINE):
        gate_keep[2 * d : 2 * d + 2, :] = gate_ref[2 * d + core]
        gate_send[2 * d : 2 * d + 2, :] = gate_ref[2 * d + 1 - core]
        for target, who in ((keep_ref, core), (send_ref, 1 - core)):
            lanes = pl.ds(pl.multiple_of((2 * d + who) * 2 * HEAD, 2 * HEAD), 2 * HEAD)
            for n, source in enumerate(sources):
                target[n, :, 2 * d * HEAD : 2 * (d + 1) * HEAD] = source[:, lanes]


def turn_kernel(x_ref, out_ref, hold):
    for j in range(x_ref.shape[1] // TOK):
        hold[j * TOK : (j + 1) * TOK, :] = x_ref[:, j * TOK : (j + 1) * TOK].T
    count, near = out_ref.shape[1:3]
    for j in range(count):
        for core in range(2):
            out_ref[core, j] = hold[(2 * j + core) * near : (2 * j + core + 1) * near, :]


def pair_kernel(place_ref, keep_ref, other_ref, out_ref):
    first = place_ref[1] == 0
    for half in range(2):
        keep, other = keep_ref[half], other_ref[half]
        out_ref[half, :, :TOK] = jnp.where(first, keep, other)
        out_ref[half, :, TOK:] = jnp.where(first, other, keep)


def other_kernel(place_ref, block_ref, out_ref):
    out_ref[...] = block_ref[1 - place_ref[1]]


def join(core, n, keep_ref, other_ref, out_ref):
    out_ref[pl.ds(pl.multiple_of(core * TOK, TOK), TOK), :] = keep_ref[n]
    out_ref[pl.ds(pl.multiple_of((1 - core) * TOK, TOK), TOK), :] = other_ref[n]


def states_kernel(place_ref, bounds_ref, *refs):
    gate_keep, gate_other, keep_ref, other_ref = refs[:4]
    out_refs, refs = refs[4 : 4 + SPAN], refs[4 + SPAN :]
    cum_ref, q_ref, g_ref, k_ref, v_ref, hold = refs
    begin, core = place_ref[0], place_ref[1]
    for n, ref in enumerate((q_ref, g_ref, k_ref, v_ref)):
        join(core, n, keep_ref, other_ref, ref)
    gates = (gate_keep[...], gate_other[...])
    swap = core == 1
    gate = jnp.concatenate(
        [jnp.where(swap, gates[1], gates[0]), jnp.where(swap, gates[0], gates[1])], axis=1
    )
    before = lax.broadcasted_iota(jnp.int32, (PAIR, PAIR), 0)
    after = lax.broadcasted_iota(jnp.int32, (PAIR, PAIR), 1)
    cum = jnp.dot(
        gate,
        (before <= after).astype(F32),
        precision=lax.Precision.HIGHEST,
        preferred_element_type=F32,
    )
    for d in range(LINE):
        cum_ref[d] = cum[2 * d : 2 * d + 2, :]
    enter = enter_columns(cum.T, bounds_ref, begin)
    leave = leave_columns(cum.T, bounds_ref, begin)
    rows = lax.broadcasted_iota(jnp.int32, (TAIL, HEAD), 0)
    for o in range(SPAN):
        tail = jnp.zeros((TAIL, HEAD), F32)
        for j in range(PART):
            h = o * PART + j
            weighted = (enter[:, h : h + 1] * q_ref[:, head_cut(h)].astype(F32)).astype(BF16)
            hold[o, head_cut(j), :] = mm(weighted, g_ref[:, head_cut(h)], 0, 0).astype(BF16)
            weighted = (leave[:, h : h + 1] * k_ref[:, head_cut(h)].astype(F32)).astype(BF16)
            hold[o, head_cut(PART + j), :] = mm(weighted, v_ref[:, head_cut(h)], 0, 0).astype(BF16)
            tail = jnp.where(rows == j, enter[PAIR - 1 :, h : h + 1], tail)
        hold[o, 2 * STATE :, :] = tail.astype(BF16)
    send_apart(place_ref[3], hold, out_refs)


def columns_of(cum_ref):
    return jnp.concatenate([cum_ref[d] for d in range(cum_ref.shape[0])], axis=0).T


def send_apart(place, hold, out_refs):
    for step, out_ref in enumerate(out_refs):
        out_ref[...] = hold[lax.rem(place + step, len(out_refs))]


def advance(state, hold, block, backward):
    pieces = []
    for j in range(PART):
        through = hold[block, 2 * STATE + j : 2 * STATE + j + 1, :].astype(F32)
        part = hold[block, head_cut(j if backward else PART + j), :].astype(F32)
        pieces.append(through * state[head_cut(j)] + part)
    return jnp.concatenate(pieces, axis=0)


def walk(backward):
    return reversed(range(SPAN)) if backward else range(SPAN)


def total_kernel(place_ref, *refs):
    parts, (back_ref, front_ref, sorted_ref) = refs[:SPAN], refs[SPAN:]
    take_in(place_ref[3], parts, sorted_ref)
    for backward, total_ref in ((True, back_ref), (False, front_ref)):
        state = jnp.zeros((STATE, HEAD), F32)
        for block in walk(backward):
            state = advance(state, sorted_ref, block, backward)
        total_ref[...] = state.astype(BF16)


def carry_kernel(place_ref, sorted_ref, back_ref, front_ref, *refs):
    out_refs, hold = refs[:SPAN], refs[SPAN]
    for backward, entry_ref in ((True, back_ref), (False, front_ref)):
        state = entry_ref[...].astype(F32)
        cut = slice(0, STATE) if backward else slice(STATE, 2 * STATE)
        for block in walk(backward):
            hold[block, cut, :] = state.astype(BF16)
            state = advance(state, sorted_ref, block, backward)
    send_apart(place_ref[3], hold, out_refs)


def take_in(lane, parts, hold):
    for step, part in enumerate(parts):
        hold[lax.rem(lane - step + SPAN, SPAN)] = part[...]


def inner_kernel(place_ref, bounds_ref, cum_ref, *refs):
    q_ref, k_ref, v_ref, g_ref, query_ref, key_ref, value_ref = refs
    begin = place_ref[0]
    cum = cum_ref[...]
    cum_t = cum.T
    row = lax.broadcasted_iota(jnp.int32, (PAIR, PAIR), 0)
    column = lax.broadcasted_iota(jnp.int32, (PAIR, PAIR), 1)
    row_ids = segment_of(bounds_ref, begin + lax.broadcasted_iota(jnp.int32, (PAIR, 1), 0))
    column_ids = segment_of(bounds_ref, begin + lax.broadcasted_iota(jnp.int32, (1, PAIR), 1))
    causal = (row >= column) & (row_ids == column_ids)
    for h in range(cum.shape[0]):
        cut = head_cut(h)
        decay = jnp.exp(jnp.where(causal, cum_t[:, h : h + 1] - cum[h : h + 1, :], -1e30))
        q, k, v, g = q_ref[:, cut], k_ref[:, cut], v_ref[:, cut], g_ref[:, cut]
        score_grad = (decay * mm(g, v, 1, 1)).astype(BF16)
        score_keys = (decay * mm(q, k, 1, 1)).astype(BF16)
        query_ref[:, cut] = mm(score_grad, k, 1, 0)
        key_ref[:, cut] = mm(score_grad, q, 0, 0)
        value_ref[:, cut] = mm(score_keys, g, 0, 0)


def piece_of(parts, h):
    for low, high, part in zip(CUTS, CUTS[1:], parts):
        if low <= h // 2 < high:
            return part[:, head_cut(h - 2 * low)]


def value_kernel(place_ref, bounds_ref, cum_ref, k_ref, *refs):
    value_in, states, refs = refs[:2], refs[2 : 2 + SPAN], refs[2 + SPAN :]
    send_ref, keep_ref, hold, out_hold = refs
    core, deep = place_ref[1], place_ref[2]
    take_in(place_ref[3], states, hold)
    leave = leave_columns(columns_of(cum_ref), bounds_ref, place_ref[0])
    for h in range(OWN):
        state = hold[h // PART, head_cut(h % PART), :]
        extra = leave[:, h : h + 1] * mm(k_ref[:, head_cut(h)], state, 1, 0)
        out_hold[h // 2, :, head_cut(h % 2)] = (piece_of(value_in, h) + extra).astype(BF16)
    keep_ref[LINE // 2 - 1] = out_hold[deep]
    send_ref[LINE // 2 - 1] = out_hold[deep]
    keep_ref[LINE // 2] = out_hold[lax.rem(deep + LINE // 2, LINE)]
    for n in range(LINE // 2 - 1):
        ahead, behind = lax.rem(deep + 1 + n, LINE), lax.rem(deep + LINE - 1 - n, LINE)
        keep_ref[n] = out_hold[jnp.where(core == 0, ahead, behind)]
        send_ref[n] = out_hold[jnp.where(core == 0, behind, ahead)]


def bundle_kernel(keep_ref, other_ref, *out_refs):
    for n, out_ref in enumerate(out_refs[:-1]):
        out_ref[0] = keep_ref[n]
        out_ref[1] = other_ref[n]
    out_refs[-1][...] = keep_ref[len(out_refs) - 1]


def part_rows(core, value, cut, keep_ref, send_ref):
    keep_ref[:, cut] = jnp.where(core == 0, value[:TOK], value[TOK:]).astype(BF16)
    send_ref[:, cut] = jnp.where(core == 0, value[TOK:], value[:TOK]).astype(BF16)


def key_kernel(place_ref, bounds_ref, cum_ref, v_ref, *refs):
    key_in, states, (keep_ref, send_ref, hold) = refs[:2], refs[2 : 2 + SPAN], refs[2 + SPAN :]
    take_in(place_ref[3], states, hold)
    leave = leave_columns(columns_of(cum_ref), bounds_ref, place_ref[0])
    for h in range(OWN):
        state = hold[h // PART, head_cut(h % PART), :]
        extra = leave[:, h : h + 1] * mm(v_ref[:, head_cut(h)], state, 1, 1)
        part_rows(place_ref[1], piece_of(key_in, h) + extra, head_cut(h), keep_ref, send_ref)


def query_kernel(place_ref, bounds_ref, cum_ref, g_ref, *refs):
    query_in, states, (keep_ref, send_ref, hold) = refs[:2], refs[2 : 2 + SPAN], refs[2 + SPAN :]
    take_in(place_ref[3], states, hold)
    enter = enter_columns(columns_of(cum_ref), bounds_ref, place_ref[0])
    for h in range(OWN):
        state = hold[h // PART, head_cut(PART + h % PART), :]
        extra = enter[:, h : h + 1] * mm(g_ref[:, head_cut(h)], state, 1, 1)
        part_rows(place_ref[1], piece_of(query_in, h) + extra, head_cut(h), keep_ref, send_ref)


def lay_kernel(place_ref, keep_ref, other_ref, *refs):
    first, out_ref, wide = place_ref[1] == 0, refs[-1], 2 * HEAD
    for d in range(keep_ref.shape[1] // wide):
        near = slice(d * wide, (d + 1) * wide)
        keep, other = keep_ref[:, near], other_ref[:, near]
        out_ref[:, 2 * d * wide : (2 * d + 1) * wide] = jnp.where(first, keep, other)
        out_ref[:, (2 * d + 1) * wide : 2 * (d + 1) * wide] = jnp.where(first, other, keep)


def by_core(place_ref, keep, other):
    first = place_ref[1] == 0
    return jnp.concatenate([jnp.where(first, keep, other), jnp.where(first, other, keep)], axis=1)


def part_out(place_ref, rows, right, out_refs, hold):
    first, x, y = place_ref[1] == 0, place_ref[3], place_ref[4]
    near = hold.shape[1]
    tall = SPAN * near
    for j in range(SPAN):
        cut = slice(j * tall, (j + 1) * tall)
        acc = mm(rows[0][cut, :], right[0], 1, 0)
        for row, column in zip(rows[1:], right[1:], strict=True):
            acc = acc + mm(row[cut, :], column, 1, 0)
        acc = acc.astype(BF16)
        for i in range(SPAN):
            hold[j * SPAN + i] = acc[i * near : (i + 1) * near]
    for step, out_ref in enumerate(out_refs):
        there_x, there_y = lax.rem(x + step, SPAN), lax.rem(y + step, SPAN)
        for n in range(SPAN):
            out_ref[n] = hold[jnp.where(first, n * SPAN + there_x, there_y * SPAN + n)]


def mine_kernel(place_ref, block_ref, out_ref):
    out_ref[...] = block_ref[place_ref[1]]


def weight_kernel(place_ref, *refs):
    count = LINE // 2 - 1
    own_row, heres, theres, refs = refs[0], refs[1 : 1 + count], refs[1 + count : 1 + 2 * count], refs[1 + 2 * count :]
    far_row, far, far_other = refs[:3]
    own, near_refs, refs = refs[3], refs[4 : 4 + 2 * count], refs[4 + 2 * count :]
    core = place_ref[1]
    rows, right = [own_row.at[core]], [by_core(place_ref, own[0], own[1])]
    for n in range(count):
        here, there = near_refs[2 * n], near_refs[2 * n + 1]
        rows += [heres[n].at[core], theres[n]]
        right.append(by_core(place_ref, here[0], here[1]))
        right.append(by_core(place_ref, there[1], there[0]))
    rows.append(far_row)
    right.append(by_core(place_ref, far[...], far_other[...]))
    part_out(place_ref, rows, right, refs[:SPAN], refs[SPAN])


def halfway_kernel(place_ref, *refs):
    parts, out_refs, hold = refs[:SPAN], refs[SPAN : 2 * SPAN], refs[2 * SPAN]
    for n in range(SPAN):
        total = parts[0][n].astype(F32)
        for part in parts[1:]:
            total = total + part[n].astype(F32)
        hold[n] = total.astype(BF16)
    send_apart(jnp.where(place_ref[1] == 0, place_ref[4], place_ref[3]), hold, out_refs)


def sum_kernel(*refs):
    parts, out_ref = refs[:-1], refs[-1]
    total = parts[0][...].astype(F32)
    for part in parts[1:]:
        total = total + part[...].astype(F32)
    out_ref[...] = total.astype(out_ref.dtype)


def shape(dims, dtype=BF16):
    return jax.ShapeDtypeStruct(dims, dtype)


def cost(heavy=0):
    return pl.CostEstimate(
        flops=1 << heavy, bytes_accessed=1, transcendentals=0
    )


def held(values, after):
    spec = pl.BlockSpec(memory_space=pl.ANY)
    return pl.pallas_call(
        lambda *refs: None,
        in_specs=[spec] * (len(values) + len(after)),
        out_specs=[spec] * len(values),
        out_shape=[shape(v.shape, v.dtype) for v in values],
        input_output_aliases={n: n for n in range(len(values))},
        compiler_params=pltpu.CompilerParams(vmem_limit_bytes=VMEM_LIMIT),
        cost_estimate=cost(),
    )(*values, *after)


def whole(kernel, smem, arrays, outs, scratch=(), after=(), heavy=0):
    vmem = pl.BlockSpec(memory_space=pltpu.VMEM)
    count = len(smem) + len(arrays)

    def body(*refs):
        kernel(*refs[:count], *refs[count + len(after) :])

    return pl.pallas_call(
        body,
        in_specs=[pl.BlockSpec(memory_space=pltpu.SMEM)] * len(smem)
        + [vmem] * len(arrays)
        + [pl.BlockSpec(memory_space=pl.ANY)] * len(after),
        out_specs=[vmem] * len(outs),
        out_shape=outs,
        scratch_shapes=list(scratch),
        compiler_params=pltpu.CompilerParams(vmem_limit_bytes=VMEM_LIMIT),
        cost_estimate=cost(heavy),
    )(*smem, *arrays, *after)


def inner(part, smem, cum, arrays, after):
    low, high = CUTS[part], CUTS[part + 1]
    outs = [shape((PAIR, (high - low) * 2 * HEAD), F32)] * 3
    count = len(smem) + 1 + len(arrays)

    def body(*refs):
        inner_kernel(*refs[:count], *refs[count + len(after) :])

    return pl.pallas_call(
        body,
        grid=(high - low,),
        in_specs=[pl.BlockSpec(memory_space=pltpu.SMEM)] * len(smem)
        + [pl.BlockSpec((None, 2, PAIR), lambda d: (d + low, 0, 0))]
        + [pl.BlockSpec((PAIR, 2 * HEAD), lambda d: (0, d + low))] * len(arrays)
        + [pl.BlockSpec(memory_space=pl.ANY)] * len(after),
        out_specs=[pl.BlockSpec((PAIR, 2 * HEAD), lambda d: (0, d))] * len(outs),
        out_shape=outs,
        compiler_params=pltpu.CompilerParams(vmem_limit_bytes=VMEM_LIMIT),
        cost_estimate=cost(WEIGHTS[part]),
    )(*smem, cum, *arrays, *after)


def lay(place, keep, other, after, heavy):
    steps = 4
    wide = keep.shape[1] // steps
    block = pl.BlockSpec((TOK, wide), lambda i: (0, i))
    return pl.pallas_call(
        lay_kernel,
        grid=(steps,),
        in_specs=[pl.BlockSpec(memory_space=pltpu.SMEM), block, block]
        + [pl.BlockSpec(memory_space=pl.ANY)] * len(after),
        out_specs=pl.BlockSpec((TOK, 2 * wide), lambda i: (0, i)),
        out_shape=shape((TOK, 2 * keep.shape[1])),
        compiler_params=pltpu.CompilerParams(vmem_limit_bytes=VMEM_LIMIT),
        cost_estimate=cost(heavy),
    )(place, keep, other, *after)


def shifted(value, axis, step):
    count = lax.axis_size(axis)
    return lax.ppermute(value, axis, [(i, (i + step) % count) for i in range(count)])


def swapped(value):
    return shifted(value, "core", 1)


def exchange(pieces, axis):
    return [pieces[0]] + [shifted(pieces[s], axis, s) for s in range(1, len(pieces))]


def apart(value, axes, moves):
    sizes = [lax.axis_size(a) for a in axes]
    pairs = []
    for place in itertools.product(*map(range, sizes)):
        for core, move in enumerate(moves):
            there = [(p + m) % n for p, m, n in zip(place, move, sizes, strict=True)]
            index = lambda at: functools.reduce(lambda t, pn: t * pn[1] + pn[0], zip(at, sizes), 0)
            pairs.append((2 * index(place) + core, 2 * index(there) + core))
    return lax.ppermute(value, (*axes, "core"), pairs)


def per_device(inputs, queries, keys, values, out_grad, log_gate, boundaries):
    q, k, v, g = queries[0], keys[0], values[0], out_grad[0]
    width = q.shape[1]
    model = inputs.shape[2]
    core, x, y = lax.axis_index("core"), lax.axis_index("x"), lax.axis_index("y")
    begin = (y * lax.axis_size("x") + x) * PAIR
    place = jnp.stack([begin, core, lax.axis_index("z"), x, y]).astype(jnp.int32)
    smem = (place, boundaries[0])
    plane = lax.axis_size("y") * lax.axis_size("x")
    count = lax.axis_size("y")
    half, chip = shape((TOK, width // 2)), shape((PAIR, width // 2))
    gate_half, cums = shape((OWN, TOK), F32), shape((LINE, 2, PAIR), F32)
    state, span = shape((STATE, HEAD)), (SPAN, 2 * STATE + TAIL, HEAD)
    hold_states = pltpu.VMEM((SPAN, 2 * STATE, HEAD), BF16)

    line = shape((2, plane, model // plane // 2, TOK))
    (turned,) = whole(turn_kernel, (), [inputs[0]], [line], [pltpu.VMEM((model, TOK), BF16)])
    turned_other = swapped(turned)
    (own,) = whole(
        pair_kernel,
        (place,),
        [a.reshape(2, model // 2, TOK) for a in (turned, turned_other)],
        [shape((2, model // 2, PAIR))],
    )
    step = lambda block: apart(block, ("z",), [(1,), (-1,)])
    ring_1 = step(own)
    gate_keep, gate_send, keep, send = whole(
        pick_kernel,
        (place,),
        [log_gate[0].reshape(OWN, 2, TOK), q, g, k, v],
        [gate_half] * 2 + [shape((4, *half.shape))] * 2,
        after=[own],
        heavy=HEAVY,
    )
    *parts, cum, q, g, k, v = whole(
        states_kernel,
        smem,
        [gate_keep, swapped(gate_send), keep, swapped(send)],
        [shape(span[1:])] * SPAN + [cums] + [chip] * 4,
        [pltpu.VMEM(span, BF16)],
    )
    parts = exchange(parts, "x")
    inner_1 = inner(0, smem, cum, [q, k, v, g], [])
    parts = held(parts, [inner_1[0]])
    (ring_1,) = held([ring_1], [parts[1]])
    ring_2 = step(ring_1)
    back, front, parts = whole(total_kernel, (place,), parts, [state, state, shape(span)])
    back = lax.ppermute(back, "y", [(i + 1, i) for i in range(count - 1)])
    front = lax.ppermute(front, "y", [(i, i + 1) for i in range(count - 1)])
    carried = whole(
        carry_kernel,
        (place,),
        [parts, back, front],
        [shape((2 * STATE, HEAD))] * SPAN,
        [hold_states],
    )
    inner_2 = inner(1, smem, cum, [q, k, v, g], [carried[0]])
    carried = exchange(carried, "x")
    (ring_2,) = held([ring_2], [inner_2[0]])
    ring_3 = step(ring_2)
    carried = held(carried, [ring_2])
    query_in, key_in, value_in = zip(inner_1, inner_2)
    several = [shape((n, PAIR, 2 * HEAD)) for n in (LINE // 2, LINE // 2 + 1)]
    send, keep = whole(
        value_kernel,
        smem,
        [cum, k, *value_in, *carried],
        several,
        [hold_states, pltpu.VMEM((LINE, PAIR, 2 * HEAD), BF16)],
        heavy=HEAVY,
    )
    *bundles, own_part, far_part = whole(
        bundle_kernel,
        (),
        [keep, swapped(send)],
        [shape((2, PAIR, 2 * HEAD))] * (LINE // 2) + [shape((PAIR, 2 * HEAD))],
    )
    started = bundles[0]
    bundles = [apart(b, ("z",), [(n + 1,), (-n - 1,)]) for n, b in enumerate(bundles)]
    far_part = apart(far_part, ("z",), [(LINE // 2,), (LINE // 2,)])
    key_keep, key_send = whole(
        key_kernel,
        smem,
        [cum, v, *key_in, *carried],
        [half] * 2,
        [hold_states],
        after=[started],
        heavy=29,
    )
    key_other = swapped(key_send)
    near = model // plane // 2
    pieces = [shape((SPAN, near, 4 * HEAD))] * SPAN
    hold_rows = pltpu.VMEM((plane, near, 4 * HEAD), BF16)
    (mine,) = whole(
        mine_kernel, (place,), [ring_3], [shape((model // 2, PAIR))], after=[key_send]
    )
    ring_4 = step(mine)

    def one_way(parts):
        moved = [apart(parts[n], ("y", "x"), [(0, n), (n, 0)]) for n in range(1, SPAN)]
        return [parts[0], *moved]

    def other_way(parts):
        moved = [apart(parts[n], ("y", "x"), [(n, 0), (0, n)]) for n in range(1, SPAN)]
        return [parts[0], *moved]

    def halfway(parts):
        return whole(
            halfway_kernel,
            (place,),
            parts,
            [shape((near, 4 * HEAD))] * SPAN,
            [pltpu.VMEM((SPAN, near, 4 * HEAD), BF16)],
        )

    rings = [ring_1, ring_2, ring_3]
    others = [
        swapped(whole(other_kernel, (place,), [r], [shape((model // 2, PAIR))])[0]) for r in rings
    ]
    columns = [own_part]
    for b in bundles:
        columns += [b, swapped(b)]
    parts = whole(
        weight_kernel,
        (place,),
        [own, *rings, *others, ring_4, far_part, swapped(far_part), *columns],
        pieces,
        [hold_rows],
        after=[key_send],
    )
    started = parts[0]
    parts = one_way(parts)
    query_keep, query_send = whole(
        query_kernel,
        smem,
        [cum, g, *query_in, *carried],
        [half] * 2,
        [hold_states],
        after=[started],
        heavy=HEAVY,
    )
    query_other = swapped(query_send)
    key_grad = lay(place, key_keep, key_other, [started], HEAVY)
    parts = halfway(held(parts, [key_grad]))
    started = parts[0]
    parts = other_way(parts)
    query_grad = lay(place, query_keep, query_other, [started], HEAVY)
    parts = held(parts, [query_grad])
    (weight,) = whole(sum_kernel, (), parts, [shape((near, 4 * HEAD), F32)])
    return query_grad[None], key_grad[None], weight


def solution(mesh):
    fine = Mesh(mesh.devices.reshape(LINE, 4, SPAN, 2), ("z", "y", "x", "core"))
    rows = P("z", CTX, None)
    in_specs = (rows, rows, rows, rows, rows, P("z", None, CTX), P("z", None))
    out_specs = (rows, rows, P(CTX, "z"))
    return jax.shard_map(
        per_device, mesh=fine, in_specs=in_specs, out_specs=out_specs, check_vma=False
    )
```
